32 devices in a mesh: date: 8 (over y, x, core), tile: 4 (over z).
Axes of the slice: x: 2, y: 2, z: 4, core: 2. Of those that a mesh axis runs over, the one named last changes fastest.
Arguments:
- reflectance: bfloat16 [2, 1024, 32, 512], P(None, 'date', 'tile'), may hold values from -6 to 6
- clear_sky: int32 [1024, 32, 4], P('date', 'tile'), may hold values 0 or 1
- harmonics: int32 [256], replicated, may hold values from 1 to 511, as said below
Outputs:
- anomaly: float32 [2, 1024, 32, 512], P(None, 'date', 'tile')
The draws below stay inside these ranges and needn't reach their ends.
Inputs may be any that keep to these rules, and one draw needn't show every extreme that they name: `harmonics`: 256 distinct frequencies; 1 and 511 are always among them.
All inputs are finite; a program needn't handle non-finite values. No bound on the sum of `clear_sky` on one device may be relied on, other than what follows from the above.
Results may differ from the reference program's by a relative error of at most 0.0012.
Values may be sent and summed in bfloat16 or wider, within the bound.
No kernel may reach another device: no remote copies, remote signals or barrier semaphores. Data moves between devices by JAX's collectives and lax.ppermute only.
A program may use at most 64 MiB of HBM per device.

```python
import jax
import jax.numpy as jnp
from jax import lax

DATES = 1024
BANDS = 2
COLS = 512
BLOCK = 128
KEEP = 256
ROWS_DEV = 8
ROWS = 32
N_TILE = 4


def draw_harmonics(key, part):
    first_key = jax.random.fold_in(key, 11)
    second_key = jax.random.fold_in(key, 23)
    middle = jax.random.permutation(first_key, DATES // 2 - 3).astype(jnp.int32) + 2
    ends = jnp.array([1, DATES // 2 - 1], dtype=jnp.int32)
    chosen = jnp.concatenate([ends, middle[:KEEP - 2]])
    return jax.random.permutation(second_key, chosen).astype(jnp.int32)


def touch_ends(entries, key, smallest, high):
    longest = entries.shape.index(max(entries.shape))
    spots = []
    for shift in (0, 1):
        where = [jax.random.randint(jax.random.fold_in(key, axis), (), 0, length) for axis, length in enumerate(entries.shape)]
        where[longest] = (where[longest] + shift) % entries.shape[longest]
        spots.append(tuple(where))
    return entries.at[spots[0]].set(smallest).at[spots[1]].set(high)


def shard_levels(rng, dims, pieces, low, largest):
    gain = 1.0
    for axis_at, parts in pieces:
        heights = jax.random.uniform(jax.random.fold_in(jax.random.fold_in(rng, 6), axis_at), (parts,), jnp.float32, low / len(pieces), largest / len(pieces))
        gain = gain * jnp.repeat(jnp.exp(heights), dims[axis_at] // parts).reshape((-1,) + (1,) * (len(dims) - 1 - axis_at))
    return gain


def gaussian(rng, shape, spread, limit, split=(), held_as=jnp.bfloat16):
    values = jax.random.normal(rng, shape, jnp.float32) * spread
    if len(split) > 0:
        values = shard_levels(rng, shape, split, -0.22, 0.18) * values
    return jnp.clip(values, min=-limit, max=limit).astype(held_as)


def setup_inputs(seed: int = 0) -> dict:
    arg_keys = jax.random.split(jax.random.key(seed), 4)
    return {
        "reflectance": gaussian(arg_keys[0], (BANDS, DATES, ROWS, COLS), 1.0, 6.0, ((1, 8), (2, 4))),
        "clear_sky": touch_ends((jax.random.randint(arg_keys[1], (DATES, ROWS, COLS // BLOCK), 0, 4) < 3).astype(jnp.int32), jax.random.fold_in(arg_keys[1], 1), 0, 1),
        "harmonics": draw_harmonics(jax.random.fold_in(arg_keys[3], 71), 0),
    }


def box_sum(field):
    widths = [(0, 0)] * (field.ndim - 1) + [(1, 1)]
    padded = jnp.pad(field, widths)
    across = padded[..., :-2] + padded[..., 1:-1] + padded[..., 2:]
    return across[..., :-2, :] + across[..., 1:-1, :] + across[..., 2:, :]


def reference(reflectance, clear_sky, harmonics):
    padded_refl = jnp.pad(reflectance, ((0, 0), (0, 0), (1, 1), (0, 0)))
    padded_sky = jnp.pad(clear_sky, ((0, 0), (1, 1), (0, 0)))
    freq = jnp.arange(DATES, dtype=jnp.int32)
    keep = jnp.sum((freq[:, None] == harmonics[None, :]).astype(jnp.float32), axis=1)

    def one_block(index):
        start = (index * ROWS_DEV).astype(jnp.int32)
        refl = lax.dynamic_slice_in_dim(padded_refl, start, ROWS_DEV + 2, 2)
        sky = lax.dynamic_slice_in_dim(padded_sky, start, ROWS_DEV + 2, 1)
        cover = jnp.repeat(sky.astype(jnp.float32), BLOCK, axis=2)
        count = box_sum(cover)
        weighted = box_sum(refl.astype(jnp.float32) * cover[None])
        smoothed = (weighted / jnp.maximum(count, 1.0)[None]).astype(jnp.bfloat16)
        spectrum = jnp.fft.fft(smoothed.astype(jnp.float32), axis=1)
        spectrum = spectrum * keep[None, :, None, None]
        seasonal = (2.0 * jnp.real(jnp.fft.ifft(spectrum, axis=1))).astype(jnp.bfloat16)
        seasonal = lax.optimization_barrier(seasonal).astype(jnp.float32)
        inner_cover = cover[:, 1:-1, :]
        inner_refl = refl[:, :, 1:-1, :].astype(jnp.float32)
        return (inner_cover[None] * (inner_refl - seasonal)).astype(jnp.float32)

    blocks = lax.map(one_block, jnp.arange(N_TILE, dtype=jnp.int32))
    return jnp.transpose(blocks, (1, 2, 0, 3, 4)).reshape(BANDS, DATES, ROWS, COLS)
```

```python
import functools
import math

import jax
import jax.numpy as jnp
from jax import lax
from jax.experimental import pallas as pl
from jax.experimental.pallas import tpu as pltpu
from jax.sharding import PartitionSpec as P

LANES = 128
SUB = 16
MIB = 2**20
DATE, TILE = ("date", "tile")


def block_spec(shape, axis):
    return pl.BlockSpec(shape, lambda i: tuple(i if d == axis else 0 for d in range(len(shape))))


def spread(small, width):
    return jnp.concatenate(
        [jnp.broadcast_to(small[:, k : k + 1], (small.shape[0], LANES)) for k in range(width)], axis=1
    )


def smooth_kernel(rows, units, has_halo, gives_edges, *refs):
    refl_ref, clear_ref = refs[:2]
    refs = refs[2:]
    if has_halo:
        before_ref, after_ref = refs[:2]
        refs = refs[2:]
    peers = lax.axis_size(DATE)
    pieces, refs = refs[:peers], refs[peers:]
    if gives_edges:
        first_ref, last_ref = refs[:2]
        refs = refs[2:]
    wide, table = refs
    bands, dates, height, cols = refl_ref.shape
    blocks = cols // LANES
    flat = bands * blocks
    me = lax.axis_index(DATE)
    lane = lax.broadcasted_iota(jnp.int32, (SUB, LANES), 1)
    none = jnp.zeros((SUB, LANES), jnp.float32)

    @pl.loop(0, dates // SUB)
    def _(step):
        at = pl.multiple_of(step * SUB, SUB)
        clear = clear_ref[pl.ds(pl.multiple_of(at * height, SUB * height), SUB * height), :].astype(jnp.float32)
        cover = spread(clear, blocks)
        for k in range(blocks):
            wide[flat + k] = cover[:, k * LANES : (k + 1) * LANES]
        for b in range(bands):
            masked = refl_ref[b, pl.ds(at, SUB)].astype(jnp.float32).reshape(SUB * height, cols) * cover
            for k in range(blocks):
                wide[b * blocks + k] = masked[:, k * LANES : (k + 1) * LANES]

        held = {}

        def get(q):
            if q not in held:
                if 0 <= q < height:
                    held[q] = [wide[n, pl.ds(q, SUB, stride=height), :] for n in range(flat + blocks)]
                else:
                    ref = before_ref if q < 0 else after_ref
                    held[q] = [ref[n, pl.ds(at, SUB), :].astype(jnp.float32) for n in range(flat)]
                    flags = ref[flat, pl.ds(at, SUB), :].astype(jnp.float32)
                    held[q] += [jnp.broadcast_to(flags[:, k : k + 1], (SUB, LANES)) for k in range(blocks)]
            return held[q]

        for i, r in enumerate(rows):
            down = [x + y + z for x, y, z in zip(get(r - 1), get(r), get(r + 1))]
            clear = [none] + down[flat:] + [none]
            for k in range(blocks):
                west = jnp.where(lane == 0, clear[k], clear[k + 1])
                east = jnp.where(lane == LANES - 1, clear[k + 2], clear[k + 1])
                scale = 1.0 / jnp.maximum(clear[k + 1] + west + east, 1.0)
                for b in range(bands):
                    n = b * blocks + k
                    west = pltpu.roll(down[n], 1, 1)
                    west = jnp.where(lane == 0, pltpu.roll(down[n - 1], 1, 1) if k > 0 else 0.0, west)
                    east = pltpu.roll(down[n], LANES - 1, 1)
                    last = k == blocks - 1
                    east = jnp.where(
                        lane == LANES - 1, 0.0 if last else pltpu.roll(down[n + 1], LANES - 1, 1), east
                    )
                    part = (down[n] + west + east) * scale
                    table[n * len(rows) + i, pl.ds(at, SUB), :] = part.astype(jnp.bfloat16)
        if gives_edges:
            for q, ref in ((0, first_ref), (height - 1, last_ref)):
                values = get(q)
                for n in range(flat):
                    ref[n, pl.ds(at, SUB), :] = values[n].astype(jnp.bfloat16)
                flags = none
                for k in range(blocks):
                    flags = jnp.where(lane == k, values[flat + k], flags)
                ref[flat, pl.ds(at, SUB), :] = flags.astype(jnp.bfloat16)

    for k in range(peers):
        pieces[k][...] = table[pl.ds((me ^ k) * units, units)]


def smooth(refl, clear, halo, rows, peers, gives_edges):
    bands, dates, height, cols = refl.shape
    blocks = cols // LANES
    number = bands * blocks * len(rows)
    units = number // peers
    depth = max(dates // 2, SUB)
    count = bands * blocks + 1
    specs = [block_spec((bands, depth, height, cols), 1), block_spec((depth * height, blocks), 0)]
    specs += [block_spec((count, depth, LANES), 1)] * len(halo)
    shapes = [jax.ShapeDtypeStruct((units, dates, LANES), jnp.bfloat16)] * peers
    out_specs = [block_spec((units, depth, LANES), 1)] * peers
    if gives_edges:
        shapes += [jax.ShapeDtypeStruct((count, dates, LANES), jnp.bfloat16)] * 2
        out_specs += [block_spec((count, depth, LANES), 1)] * 2
    return pl.pallas_call(
        functools.partial(smooth_kernel, rows, units, len(halo) > 0, gives_edges),
        grid=(dates // depth,),
        in_specs=specs,
        out_specs=out_specs,
        out_shape=shapes,
        scratch_shapes=[
            pltpu.VMEM(((bands + 1) * blocks, SUB * height, LANES), jnp.float32),
            pltpu.VMEM((number, depth, LANES), jnp.bfloat16),
        ],
        compiler_params=pltpu.CompilerParams(vmem_limit_bytes=24 * MIB),
        cost_estimate=pl.CostEstimate(flops=20 * number * dates * LANES, bytes_accessed=4 * MIB, transcendentals=0),
        name="smooth",
    )(refl, clear, *halo)


def filter_kernel(wave_ref, high_ref, low_ref):
    total = wave_ref.shape[1]
    wave = jnp.broadcast_to(wave_ref[0:1, :], (LANES, total))
    turned = pltpu.roll(wave, 0, 1, stride=1, stride_axis=0)
    high = turned.astype(jnp.bfloat16)
    low = (turned - high.astype(jnp.float32)).astype(jnp.bfloat16)
    for a in range(total // LANES):
        for ref, part in ((high_ref, high), (low_ref, low)):
            if a == 0:
                ref[0:LANES, :] = part
            else:
                cut = total - a * LANES
                ref[a * LANES : (a + 1) * LANES, 0 : a * LANES] = part[:, cut:]
                ref[a * LANES : (a + 1) * LANES, a * LANES :] = part[:, :cut]


def filter_matrix(harmonics, total):
    steps = jnp.arange(total, dtype=jnp.int32)
    turns = harmonics[:, None] * steps[None, :] % total
    wave = jnp.sum(jnp.cos(turns.astype(jnp.float32) * (2.0 * math.pi / total)), axis=0) * (2.0 / total)
    wave = jnp.broadcast_to(wave[None, :], (8, total))
    return pl.pallas_call(
        filter_kernel,
        out_shape=[jax.ShapeDtypeStruct((total, total), jnp.bfloat16)] * 2,
        compiler_params=pltpu.CompilerParams(vmem_limit_bytes=24 * MIB),
        name="filter_matrix",
    )(wave)


def apply_kernel(peers, high_ref, low_ref, *refs):
    pieces, outs = refs[:peers], refs[peers : 2 * peers]
    series, result = refs[2 * peers :]
    units, dates, lanes = pieces[0].shape
    total = series.shape[0]
    me = lax.axis_index(DATE)
    for k in range(peers):
        at = pl.multiple_of((me ^ k) * dates, dates)
        for i in range(units):
            series[pl.ds(at, dates), i * lanes : (i + 1) * lanes] = pieces[k][i]
    tile = min(total, 256)

    @pl.loop(0, total // tile)
    def _(step):
        at = pl.ds(pl.multiple_of(step * tile, tile), tile)
        result[at, :] = jnp.dot(high_ref[at, :], series[...], preferred_element_type=jnp.float32) + jnp.dot(
            low_ref[at, :], series[...], preferred_element_type=jnp.float32
        )

    for k in range(peers):
        at = pl.multiple_of((me ^ k) * dates, dates)
        for i in range(units):
            outs[k][i] = result[pl.ds(at, dates), i * lanes : (i + 1) * lanes].astype(jnp.bfloat16)


def apply_filter(high, low, pieces):
    peers = len(pieces)
    units, dates, lanes = pieces[0].shape
    total = dates * peers
    return pl.pallas_call(
        functools.partial(apply_kernel, peers),
        out_shape=[jax.ShapeDtypeStruct((units, dates, lanes), jnp.bfloat16)] * peers,
        scratch_shapes=[
            pltpu.VMEM((total, units * lanes), jnp.bfloat16),
            pltpu.VMEM((total, units * lanes), jnp.float32),
        ],
        compiler_params=pltpu.CompilerParams(vmem_limit_bytes=32 * MIB),
        cost_estimate=pl.CostEstimate(
            flops=4 * total * total * units * lanes, bytes_accessed=6 * MIB, transcendentals=0
        ),
        name="apply_filter",
    )(high, low, *pieces)


def anomaly_kernel(chunks, peers, refl_ref, clear_ref, *refs):
    count = len(chunks) * peers
    pieces, out_ref, (table, wide) = refs[:count], refs[count], refs[count + 1 :]
    bands, dates, height, cols = refl_ref.shape
    blocks = cols // LANES
    me = lax.axis_index(DATE)
    start = 0
    for c, rows in enumerate(chunks):
        units = pieces[c * peers].shape[0]
        for k in range(peers):
            table[pl.ds(start + (me ^ k) * units, units)] = pieces[c * peers + k][...]
        start += units * peers

    @pl.loop(0, dates // SUB)
    def _(step):
        at = pl.multiple_of(step * SUB, SUB)
        unit = 0
        for rows in chunks:
            for b in range(bands):
                for k in range(blocks):
                    for r in rows:
                        part = table[unit, pl.ds(at, SUB), :].astype(jnp.float32)
                        wide[b * blocks + k, pl.ds(r, SUB, stride=height), :] = part
                        unit += 1
        clear = clear_ref[pl.ds(pl.multiple_of(at * height, SUB * height), SUB * height), :].astype(jnp.float32)
        cover = spread(clear, blocks)
        for b in range(bands):
            held = refl_ref[b, pl.ds(at, SUB)].astype(jnp.float32).reshape(SUB * height, cols)
            base = jnp.concatenate([wide[b * blocks + k] for k in range(blocks)], axis=1)
            out_ref[b, pl.ds(at, SUB)] = (cover * (held - base)).reshape(SUB, height, cols)


def anomaly(refl, clear, chunks, pieces, peers):
    bands, dates, height, cols = refl.shape
    blocks = cols // LANES
    depth = max(dates // 4, SUB)
    specs = [block_spec((bands, depth, height, cols), 1), block_spec((depth * height, blocks), 0)]
    specs += [block_spec((p.shape[0], depth, LANES), 1) for p in pieces]
    return pl.pallas_call(
        functools.partial(anomaly_kernel, chunks, peers),
        grid=(dates // depth,),
        in_specs=specs,
        out_specs=block_spec((bands, depth, height, cols), 1),
        out_shape=jax.ShapeDtypeStruct(refl.shape, jnp.float32),
        scratch_shapes=[
            pltpu.VMEM((bands * blocks * height, depth, LANES), jnp.bfloat16),
            pltpu.VMEM((bands * blocks, SUB * height, LANES), jnp.float32),
        ],
        compiler_params=pltpu.CompilerParams(vmem_limit_bytes=32 * MIB),
        name="anomaly",
    )(refl, clear, *pieces)


def exchange(pieces):
    peers = len(pieces)
    return [pieces[0]] + [
        lax.ppermute(pieces[k], DATE, [(i, i ^ k) for i in range(peers)]) for k in range(1, peers)
    ]


def on_device(reflectance, clear_sky, harmonics):
    bands, dates, height, cols = reflectance.shape
    peers, tiles = lax.axis_size(DATE), lax.axis_size(TILE)
    clear = clear_sky.reshape(dates * height, clear_sky.shape[2])
    half = height // 2
    chunks = (tuple(range(1, half + 1)), tuple(range(half + 1, height)) + (0,))
    out = smooth(reflectance, clear, (), chunks[0], peers, True)
    inner, first, last = out[:peers], out[peers], out[peers + 1]
    up = [(i, i + 1) for i in range(tiles - 1)]
    before = lax.ppermute(last, TILE, up)
    after = lax.ppermute(first, TILE, [(j, i) for i, j in up])
    inner = exchange(inner)
    outer = exchange(smooth(reflectance, clear, (before, after), chunks[1], peers, False))
    high, low = filter_matrix(harmonics, dates * peers)
    inner = exchange(apply_filter(high, low, inner))
    outer = exchange(apply_filter(high, low, outer))
    return anomaly(reflectance, clear, chunks, inner + outer, peers)


def solution(mesh):
    return jax.shard_map(
        on_device,
        mesh=mesh,
        in_specs=(P(None, DATE, TILE, None), P(DATE, TILE, None), P()),
        out_specs=P(None, DATE, TILE, None),
        check_vma=False,
    )
```

```python
import functools
import math

import jax
import jax.numpy as jnp
from jax import lax
from jax.experimental import pallas as pl
from jax.experimental.pallas import tpu as pltpu
from jax.sharding import PartitionSpec as P

LANES = 128
SUB = 32
MIB = 2**20
DATE, TILE = ("date", "tile")


def padded(size):
    return -(-size // LANES) * LANES


def turn_flags(clear_ref, flags_in, flags):
    height, blocks, dates = clear_ref.shape
    flags_in[...] = jnp.zeros_like(flags_in)
    for q in range(height):
        flags_in[q * blocks : (q + 1) * blocks, 0:dates] = clear_ref[q].astype(jnp.float32)
    flags[...] = flags_in[...].T.astype(jnp.bfloat16)


def grid_of(shape):
    return lax.broadcasted_iota(jnp.int32, shape, 0), lax.broadcasted_iota(jnp.int32, shape, 1)


def table_of(index, values):
    out = jnp.zeros_like(index)
    for i, value in enumerate(values):
        out = jnp.where(index == i, value, out)
    return out


def as_matrix(choice):
    return jnp.where(choice, 1.0, 0.0).astype(jnp.bfloat16)


def product(left, right):
    return jnp.dot(left, right, preferred_element_type=jnp.float32)


def add_row(lines, place, extra):
    parts = [lines[i : i + SUB] for i in range(0, lines.shape[0], SUB)]
    parts[place] = parts[place] + extra
    return jnp.concatenate(parts, axis=0)


def cover_matrices(height, blocks, width):
    line, date = grid_of((SUB * height, SUB))
    repeat = as_matrix(lax.div(line, height) == date)
    line, lane = grid_of((SUB * height, width))
    own = lax.rem(line, height) == lax.div(lane, blocks)
    lane, column = grid_of((width, blocks * LANES))
    columns = as_matrix(lax.rem(lane, blocks) == lax.div(column, LANES))
    return repeat, own, columns


def box_columns(blocks, width):
    lane, column = grid_of((width, blocks * LANES))
    total = jnp.zeros(lane.shape, jnp.float32)
    for shift in (-1, 0, 1):
        at = column + shift
        there = jnp.where(at < 0, -1, lax.div(at, LANES))
        total = total + jnp.where(there == lax.rem(lane, blocks), 1.0, 0.0)
    return total.astype(jnp.bfloat16)


def flag_lines(clear, repeat, own):
    return jnp.where(own, product(repeat, clear), 0.0).astype(jnp.bfloat16)


def turn_matrix(rows, height):
    line, source = grid_of((len(rows) * SUB, SUB * height))
    apart = jnp.abs(table_of(lax.div(line, SUB), rows) - lax.rem(source, height))
    return as_matrix((lax.rem(line, SUB) == lax.div(source, height)) & (apart <= 1))


def back_matrix(rows, height):
    line, source = grid_of((SUB * height, len(rows) * SUB))
    row = table_of(lax.div(source, SUB), rows)
    return as_matrix((lax.div(line, height) == lax.rem(source, SUB)) & (lax.rem(line, height) == row))


class Shelf:
    def __init__(self, rows, height, blocks, dates):
        width = padded(height * blocks)
        lines = len(rows) * SUB
        start = dates * height
        self.box = (pl.ds(start, width), pl.ds(0, blocks * LANES))
        start += width
        self.near = [(pl.ds(start + step * lines, lines), pl.ds(0, width)) for step in range(dates // SUB)]
        self.turn = (pl.ds(start, lines), pl.ds(width, SUB * height))
        self.back = (pl.ds(start + lines, SUB * height), pl.ds(width, SUB * height))
        self.size = start + max(dates // SUB * lines, lines + SUB * height)


def smooth_lines(down, scale, lane):
    cols = down.shape[1]
    west = jnp.where(lane == 0, 0.0, pltpu.roll(down, 1, 1))
    east = jnp.where(lane == cols - 1, 0.0, pltpu.roll(down, cols - 1, 1))
    return ((down + west + east) * scale).astype(jnp.bfloat16)


def file_lines(table, at, smoothed, rows, b, bands):
    blocks = smoothed.shape[1] // LANES
    for k in range(blocks):
        for i in range(len(rows)):
            part = smoothed[i * SUB : (i + 1) * SUB, k * LANES : (k + 1) * LANES]
            table[(k * len(rows) + i) * bands + b, at, :] = part


def give_pieces(table, pieces):
    units = table.shape[0] // len(pieces)
    chip = lax.axis_index(DATE) // 2
    for m, piece in enumerate(pieces):
        piece[...] = table[pl.ds((chip ^ m) * units, units)]


def first_kernel(chunks, chips, refl_ref, clear_ref, *refs):
    pieces, refs = refs[:chips], refs[chips:]
    masked_ref, first_ref, last_ref = refs[:3]
    table, held_ref, clear_held, flags_in, flags, sems = refs[3:]
    rows, rest = chunks
    bands, lines_all, cols = refl_ref.shape
    dates = pieces[0].shape[1]
    height = lines_all // dates
    shelf_ref = masked_ref.at[bands]
    blocks = cols // LANES
    flat = bands * blocks
    width = flags.shape[1]
    shelf = Shelf(rest, height, blocks, dates)

    def fetch(step):
        at = pl.ds(step * SUB * height, SUB * height)
        return pltpu.make_async_copy(refl_ref.at[:, at], held_ref.at[:, at], sems.at[step])

    fetch_clear = pltpu.make_async_copy(clear_ref, clear_held, sems.at[dates // SUB])
    fetch_clear.start()
    for step in range(dates // SUB):
        fetch(step).start()
    line, source = grid_of((2 * SUB, SUB * height))
    edge = jnp.where(line < SUB, 0, height - 1)
    edges = as_matrix((lax.rem(line, SUB) == lax.div(source, height)) & (edge == lax.rem(source, height)))
    flag_lane = lax.broadcasted_iota(jnp.int32, (SUB, width), 1)
    repeat, own, columns = cover_matrices(height, blocks, width)
    box = box_columns(blocks, width)
    turn = turn_matrix(rows, height)
    turn_rest = turn_matrix(rest, height)
    shelf_ref[shelf.box] = box
    shelf_ref[shelf.turn] = turn_rest
    shelf_ref[shelf.back] = back_matrix(rows + rest, height)
    lane = lax.broadcasted_iota(jnp.int32, (len(rows) * SUB, cols), 1)
    fetch_clear.wait()
    turn_flags(clear_held, flags_in, flags)

    for step in range(dates // SUB):
        at = pl.ds(step * SUB, SUB)
        here = pl.ds(step * SUB * height, SUB * height)
        clear = flags[at, :]
        lines = flag_lines(clear, repeat, own)
        cover = product(lines, columns).astype(jnp.bfloat16)
        shelf_ref[here, :] = cover
        for q, ref in ((0, first_ref), (height - 1, last_ref)):
            kept = jnp.where(lax.div(flag_lane, blocks) == q, clear.astype(jnp.float32), 0.0)
            ref[flat, at, :] = kept.astype(jnp.bfloat16)
        shelf_ref[shelf.near[step]] = product(turn_rest, lines).astype(jnp.bfloat16)
        count = product(product(turn, lines).astype(jnp.bfloat16), box)
        scale = 1.0 / jnp.maximum(count, 1.0)
        fetch(step).wait()
        for b in range(bands):
            masked = held_ref[b, here, :] * cover
            masked_ref[b, here, :] = masked
            ends = product(edges, masked).astype(jnp.bfloat16)
            for i, ref in enumerate((first_ref, last_ref)):
                for k in range(blocks):
                    ref[b * blocks + k, at, :] = ends[i * SUB : (i + 1) * SUB, k * LANES : (k + 1) * LANES]
            file_lines(table, at, smooth_lines(product(turn, masked), scale, lane), rows, b, bands)
    give_pieces(table, pieces)


def smooth_first(refl, clear, chunks, chips):
    bands, lines, cols = refl.shape
    height, blocks, dates = clear.shape
    number = bands * blocks * len(chunks[0])
    width = padded(height * blocks)
    pieces = [jax.ShapeDtypeStruct((number // chips, dates, LANES), jnp.bfloat16)] * chips
    size = Shelf(chunks[1], height, blocks, dates).size
    held = [pltpu.VMEM((bands + 1, size, cols), jnp.bfloat16)]
    edges = [jax.ShapeDtypeStruct((bands * blocks + 1, dates, width), jnp.bfloat16)] * 2
    return pl.pallas_call(
        functools.partial(first_kernel, chunks, chips),
        in_specs=[pl.BlockSpec(memory_space=pltpu.HBM)] * 2,
        out_specs=[pl.BlockSpec(memory_space=pltpu.VMEM)] * (chips + 3),
        out_shape=pieces + held + edges,
        scratch_shapes=[
            pltpu.VMEM((number, dates, LANES), jnp.bfloat16),
            pltpu.VMEM(refl.shape, refl.dtype),
            pltpu.VMEM(clear.shape, clear.dtype),
            pltpu.VMEM((width, padded(dates)), jnp.float32),
            pltpu.VMEM((padded(dates), width), jnp.bfloat16),
            pltpu.SemaphoreType.DMA((dates // SUB + 1,)),
        ],
        compiler_params=pltpu.CompilerParams(vmem_limit_bytes=14 * MIB),
        name="smooth_first",
    )(pltpu.with_memory_space_constraint(refl, pltpu.HBM), pltpu.with_memory_space_constraint(clear, pltpu.HBM))


def rest_kernel(rows, chips, height, masked_ref, before_ref, after_ref, *refs):
    pieces, table = refs[:chips], refs[chips]
    bands, cols = masked_ref.shape[0] - 1, masked_ref.shape[2]
    dates = pieces[0].shape[1]
    blocks = cols // LANES
    flat = bands * blocks
    shelf_ref = masked_ref.at[bands]
    shelf = Shelf(rows, height, blocks, dates)
    halo = tuple((rows.index(q), ref) for q, ref in ((0, before_ref), (height - 1, after_ref)))
    box, turn = shelf_ref[shelf.box], shelf_ref[shelf.turn]
    lane = lax.broadcasted_iota(jnp.int32, (len(rows) * SUB, cols), 1)
    for step in range(dates // SUB):
        at = pl.ds(step * SUB, SUB)
        here = pl.ds(step * SUB * height, SUB * height)
        count = product(shelf_ref[shelf.near[step]], box)
        for place, ref in halo:
            count = add_row(count, place, product(ref[flat, at, :], box))
        scale = 1.0 / jnp.maximum(count, 1.0)
        for b in range(bands):
            down = product(turn, masked_ref[b, here, :])
            for place, ref in halo:
                extra = jnp.concatenate([ref[b * blocks + k, at, :] for k in range(blocks)], axis=1)
                down = add_row(down, place, extra.astype(jnp.float32))
            file_lines(table, at, smooth_lines(down, scale, lane), rows, b, bands)
    give_pieces(table, pieces)


def hand_on_kernel(first_in, last_in, first_out, last_out):
    first_out[...] = first_in[...]
    last_out[...] = last_in[...]


def hand_on(first, last):
    return pl.pallas_call(
        hand_on_kernel,
        out_shape=[jax.ShapeDtypeStruct(x.shape, x.dtype) for x in (first, last)],
        compiler_params=pltpu.CompilerParams(vmem_limit_bytes=8 * MIB),
        name="hand_on",
    )(first, last)


def smooth_rest(masked, height, halo, rows, chips):
    bands, cols = masked.shape[0] - 1, masked.shape[2]
    dates = halo[0].shape[1]
    number = bands * (cols // LANES) * len(rows)
    return pl.pallas_call(
        functools.partial(rest_kernel, rows, chips, height),
        in_specs=[pl.BlockSpec(memory_space=pltpu.VMEM)] * 3,
        out_shape=[jax.ShapeDtypeStruct((number // chips, dates, LANES), jnp.bfloat16)] * chips,
        scratch_shapes=[pltpu.VMEM((number, dates, LANES), jnp.bfloat16)],
        compiler_params=pltpu.CompilerParams(vmem_limit_bytes=12 * MIB),
        name="smooth_rest",
    )(masked, *halo)


def filter_kernel(dates, wave_ref, high_ref, low_ref):
    total = high_ref.shape[1]
    chips = total // dates // 2
    core = lax.axis_index(DATE) % 2
    wave = jnp.concatenate(
        [jnp.broadcast_to(wave_ref[a : a + 1, :], (dates, LANES)) for a in range(total // LANES)], axis=1
    )
    same = pltpu.roll(wave, 0, 1, stride=1, stride_axis=0)
    other = jnp.where(core == 0, pltpu.roll(same, total - dates, 1), pltpu.roll(same, dates, 1))
    for side, base in enumerate((same, other)):
        high = base.astype(jnp.bfloat16)
        low = (base - high.astype(jnp.float32)).astype(jnp.bfloat16)
        for ref, part in ((high_ref, high), (low_ref, low)):
            for q in range(chips):
                for s in range(chips):
                    at = (s - q) % chips * 2 * dates
                    left = (side * chips + s) * dates
                    ref[q * dates : (q + 1) * dates, left : left + dates] = part[:, at : at + dates]


def filter_matrix(harmonics, dates, peers):
    total = dates * peers
    fine = jnp.arange(LANES, dtype=jnp.int32)
    coarse = jnp.arange(0, total, LANES, dtype=jnp.int32)

    def turned(steps):
        angle = (harmonics[:, None] * steps[None, :] % total).astype(jnp.float32) * (2.0 * math.pi / total)
        return jnp.cos(angle), jnp.sin(angle)

    (cos_a, sin_a), (cos_b, sin_b) = turned(coarse), turned(fine)
    wave = jnp.einsum(
        "fa,fb->ab",
        jnp.concatenate([cos_a, sin_a], axis=0),
        jnp.concatenate([cos_b, -sin_b], axis=0),
        precision=lax.Precision.HIGHEST,
    )
    wave = wave * (2.0 / total)
    return pl.pallas_call(
        functools.partial(filter_kernel, dates),
        out_shape=[jax.ShapeDtypeStruct((total // 2, total), jnp.bfloat16)] * 2,
        compiler_params=pltpu.CompilerParams(vmem_limit_bytes=10 * MIB),
        name="filter_matrix",
    )(wave)


def pack_kernel(chips, *refs):
    pieces, out_ref = refs[:chips], refs[-1]
    units, dates, lanes = pieces[0].shape
    chip = lax.axis_index(DATE) // 2
    for m in range(chips):
        at = pl.multiple_of((chip ^ m) * dates, dates)
        for i in range(units):
            out_ref[pl.ds(at, dates), i * lanes : (i + 1) * lanes] = pieces[m][i]


def pack(pieces, after):
    units, dates, lanes = pieces[0].shape
    return pl.pallas_call(
        functools.partial(pack_kernel, len(pieces)),
        out_shape=jax.ShapeDtypeStruct((len(pieces) * dates, units * lanes), jnp.bfloat16),
        in_specs=[pl.BlockSpec(memory_space=pltpu.VMEM)] * len(pieces) + [pl.BlockSpec(memory_space=pl.ANY)] * len(after),
        compiler_params=pltpu.CompilerParams(vmem_limit_bytes=8 * MIB),
        name="pack",
    )(*pieces, *after)


def apply_kernel(chips, high_ref, low_ref, own_ref, other_ref, *refs):
    outs, result = refs[:chips], refs[chips]
    units, dates, lanes = outs[0].shape
    half = own_ref.shape[0]
    chip = lax.axis_index(DATE) // 2
    tile = min(half, 256)

    @pl.loop(0, half // tile)
    def _(step):
        at = pl.ds(pl.multiple_of(step * tile, tile), tile)
        total = None
        for ref in (high_ref, low_ref):
            for series, left in ((own_ref, 0), (other_ref, half)):
                part = jnp.dot(
                    ref[at, left : left + half], series[...], preferred_element_type=jnp.float32
                )
                total = part if total is None else total + part
        result[at, :] = total

    for m in range(chips):
        at = pl.multiple_of((chip ^ m) * dates, dates)
        for i in range(units):
            outs[m][i] = result[pl.ds(at, dates), i * lanes : (i + 1) * lanes].astype(jnp.bfloat16)


def apply_filter(high, low, own, other, chips):
    half, width = own.shape
    piece = jax.ShapeDtypeStruct((width // LANES, half // chips, LANES), jnp.bfloat16)
    return pl.pallas_call(
        functools.partial(apply_kernel, chips),
        out_shape=[piece] * chips,
        scratch_shapes=[pltpu.VMEM((half, width), jnp.float32)],
        compiler_params=pltpu.CompilerParams(vmem_limit_bytes=16 * MIB),
        name="apply_filter",
    )(high, low, own, other)


def anomaly_kernel(chunks, chips, masked_ref, *refs):
    count = len(chunks) * chips
    pieces, (out_ref, table, made, sems) = refs[:count], refs[count:]
    bands, lines, cols = made.shape
    shelf_ref = masked_ref.at[bands]
    dates = table.shape[1]
    height = lines // dates
    blocks = cols // LANES
    chip = lax.axis_index(DATE) // 2
    order, start = [], 0
    for c, rows in enumerate(chunks):
        units = pieces[c * chips].shape[0]
        for m in range(chips):
            table[pl.ds(start + (chip ^ m) * units, units)] = pieces[c * chips + m][...]
        order += [(r, start + i * bands, len(rows) * bands) for i, r in enumerate(rows)]
        start += units * chips

    turn = shelf_ref[Shelf(chunks[1], height, blocks, dates).back]

    def store(step, b):
        here = pl.ds(step * SUB * height, SUB * height)
        return pltpu.make_async_copy(made.at[b, here], out_ref.at[b, here], sems.at[step, b])

    for step in range(dates // SUB):
        at = pl.ds(step * SUB, SUB)
        here = pl.ds(step * SUB * height, SUB * height)
        cover = shelf_ref[here, :].astype(jnp.float32)
        for b in range(bands):
            seasonal = jnp.concatenate(
                [
                    jnp.concatenate([table[first + k * step_k + b, at, :] for k in range(blocks)], axis=1)
                    for _, first, step_k in order
                ],
                axis=0,
            )
            made[b, here, :] = masked_ref[b, here, :].astype(jnp.float32) - cover * product(turn, seasonal)
            store(step, b).start()
    for step in range(dates // SUB):
        for b in range(bands):
            store(step, b).wait()


def anomaly(masked, height, chunks, pieces, chips):
    bands, cols = masked.shape[0] - 1, masked.shape[2]
    dates = pieces[0].shape[1]
    lines = dates * height
    return pl.pallas_call(
        functools.partial(anomaly_kernel, chunks, chips),
        in_specs=[pl.BlockSpec(memory_space=pltpu.VMEM)] * (1 + len(pieces)),
        out_specs=pl.BlockSpec(memory_space=pl.ANY),
        out_shape=jax.ShapeDtypeStruct((bands, lines, cols), jnp.float32),
        scratch_shapes=[
            pltpu.VMEM((bands * cols // LANES * height, dates, LANES), jnp.bfloat16),
            pltpu.VMEM((bands, lines, cols), jnp.float32),
            pltpu.SemaphoreType.DMA((dates // SUB, bands)),
        ],
        compiler_params=pltpu.CompilerParams(vmem_limit_bytes=16 * MIB),
        name="anomaly",
    )(masked, *pieces)


def exchange(pieces, peers):
    out = list(pieces)
    for m in range(len(pieces) - 1, 0, -1):
        out[m] = lax.ppermute(pieces[m], DATE, [(i, i ^ (2 * m)) for i in range(peers)])
    return out


def on_device(reflectance, clear_sky, harmonics):
    bands, dates, height, cols = reflectance.shape
    peers, tiles = lax.axis_size(DATE), lax.axis_size(TILE)
    chips = peers // 2
    clear = jnp.transpose(clear_sky, (1, 2, 0))
    chunks = (tuple(range(1, height - 1)), (height - 1, 0))
    refl = reflectance.reshape(bands, dates * height, cols)
    out = smooth_first(refl, clear, chunks, chips)
    masked, first, last = out[chips:]
    inner = exchange(out[:chips], peers)
    first, last = hand_on(first, last)
    up = [(i, i + 1) for i in range(tiles - 1)]
    before = lax.ppermute(last, TILE, up)
    after = lax.ppermute(first, TILE, [(j, i) for i, j in up])
    edges = smooth_rest(masked, height, (before, after), chunks[1], chips)
    outer = exchange(edges, peers)
    high, low = filter_matrix(harmonics, dates, peers)
    results, after = [], [high, edges[0]]
    for pieces in (inner, outer):
        own = pack(pieces, after)
        other = lax.ppermute(own, DATE, [(i, i ^ 1) for i in range(peers)])
        made = apply_filter(high, low, own, other, chips)
        results += exchange(made, peers)
        after = [made[0]]
    return anomaly(masked, height, chunks, results, chips).reshape(reflectance.shape)


def solution(mesh):
    return jax.shard_map(
        on_device,
        mesh=mesh,
        in_specs=(P(None, DATE, TILE, None), P(DATE, TILE, None), P()),
        out_specs=P(None, DATE, TILE, None),
        check_vma=False,
    )
```

```python
import functools
import math

import jax
import jax.numpy as jnp
from jax import lax
from jax.experimental import pallas as pl
from jax.experimental.pallas import tpu as pltpu
from jax.sharding import PartitionSpec as P

LANES = 128
SUB = 32
MIB = 2**20
DATE, TILE = ("date", "tile")


def padded(size):
    return -(-size // LANES) * LANES


def turn_flags(clear_ref, flags_in, flags):
    height, blocks, dates = clear_ref.shape
    flags_in[...] = jnp.zeros_like(flags_in)
    for q in range(height):
        flags_in[q * blocks : (q + 1) * blocks, 0:dates] = clear_ref[q].astype(jnp.float32)
    flags[...] = flags_in[...].T.astype(jnp.bfloat16)


def grid_of(shape):
    return lax.broadcasted_iota(jnp.int32, shape, 0), lax.broadcasted_iota(jnp.int32, shape, 1)


def table_of(index, values):
    out = jnp.zeros_like(index)
    for i, value in enumerate(values):
        out = jnp.where(index == i, value, out)
    return out


def as_matrix(choice):
    return jnp.where(choice, 1.0, 0.0).astype(jnp.bfloat16)


def product(left, right):
    return jnp.dot(left, right, preferred_element_type=jnp.float32)


def add_row(lines, place, extra):
    parts = [lines[i : i + SUB] for i in range(0, lines.shape[0], SUB)]
    parts[place] = parts[place] + extra
    return jnp.concatenate(parts, axis=0)


def cover_matrices(height, blocks, width):
    line, date = grid_of((SUB * height, SUB))
    repeat = as_matrix(lax.div(line, height) == date)
    line, lane = grid_of((SUB * height, width))
    own = lax.rem(line, height) == lax.div(lane, blocks)
    lane, column = grid_of((width, blocks * LANES))
    columns = as_matrix(lax.rem(lane, blocks) == lax.div(column, LANES))
    return repeat, own, columns


def box_columns(blocks, width):
    lane, column = grid_of((width, blocks * LANES))
    total = jnp.zeros(lane.shape, jnp.float32)
    for shift in (-1, 0, 1):
        at = column + shift
        there = jnp.where(at < 0, -1, lax.div(at, LANES))
        total = total + jnp.where(there == lax.rem(lane, blocks), 1.0, 0.0)
    return total.astype(jnp.bfloat16)


def flag_lines(clear, repeat, own):
    return jnp.where(own, product(repeat, clear), 0.0).astype(jnp.bfloat16)


def turn_matrix(rows, height):
    line, source = grid_of((len(rows) * SUB, SUB * height))
    apart = jnp.abs(table_of(lax.div(line, SUB), rows) - lax.rem(source, height))
    return as_matrix((lax.rem(line, SUB) == lax.div(source, height)) & (apart <= 1))


def back_matrix(rows, height):
    line, source = grid_of((SUB * height, len(rows) * SUB))
    row = table_of(lax.div(source, SUB), rows)
    return as_matrix((lax.div(line, height) == lax.rem(source, SUB)) & (lax.rem(line, height) == row))


class Shelf:
    def __init__(self, rows, height, blocks, dates):
        width = padded(height * blocks)
        lines = len(rows) * SUB
        start = dates * height
        self.box = (pl.ds(start, width), pl.ds(0, blocks * LANES))
        start += width
        self.near = [(pl.ds(start + step * lines, lines), pl.ds(0, width)) for step in range(dates // SUB)]
        self.turn = (pl.ds(start, lines), pl.ds(width, SUB * height))
        self.back = (pl.ds(start + lines, SUB * height), pl.ds(width, SUB * height))
        self.size = start + max(dates // SUB * lines, lines + SUB * height)


def smooth_lines(down, scale, lane):
    cols = down.shape[1]
    west = jnp.where(lane == 0, 0.0, pltpu.roll(down, 1, 1))
    east = jnp.where(lane == cols - 1, 0.0, pltpu.roll(down, cols - 1, 1))
    return ((down + west + east) * scale).astype(jnp.bfloat16)


def file_lines(table, at, smoothed, rows, b, bands):
    blocks = smoothed.shape[1] // LANES
    for k in range(blocks):
        for i in range(len(rows)):
            part = smoothed[i * SUB : (i + 1) * SUB, k * LANES : (k + 1) * LANES]
            table[(k * len(rows) + i) * bands + b, at, :] = part


def give_pieces(table, pieces):
    units = table.shape[0] // len(pieces)
    chip = lax.axis_index(DATE) // 2
    for m, piece in enumerate(pieces):
        piece[...] = table[pl.ds((chip ^ m) * units, units)]


def first_kernel(chunks, chips, refl_ref, clear_ref, *refs):
    pieces, refs = refs[:chips], refs[chips:]
    masked_ref, first_ref, last_ref = refs[:3]
    table, held_ref, clear_held, flags_in, flags, sems = refs[3:]
    rows, rest = chunks
    bands, lines_all, cols = refl_ref.shape
    dates = pieces[0].shape[1]
    height = lines_all // dates
    shelf_ref = masked_ref.at[bands]
    blocks = cols // LANES
    flat = bands * blocks
    width = flags.shape[1]
    shelf = Shelf(rest, height, blocks, dates)

    def fetch(step):
        at = pl.ds(step * SUB * height, SUB * height)
        return pltpu.make_async_copy(refl_ref.at[:, at], held_ref.at[:, at], sems.at[step])

    fetch_clear = pltpu.make_async_copy(clear_ref, clear_held, sems.at[dates // SUB])
    fetch_clear.start()
    for step in range(dates // SUB):
        fetch(step).start()
    line, source = grid_of((2 * SUB, SUB * height))
    edge = jnp.where(line < SUB, 0, height - 1)
    edges = as_matrix((lax.rem(line, SUB) == lax.div(source, height)) & (edge == lax.rem(source, height)))
    flag_lane = lax.broadcasted_iota(jnp.int32, (SUB, width), 1)
    repeat, own, columns = cover_matrices(height, blocks, width)
    box = box_columns(blocks, width)
    turn = turn_matrix(rows, height)
    turn_rest = turn_matrix(rest, height)
    shelf_ref[shelf.box] = box
    shelf_ref[shelf.turn] = turn_rest
    shelf_ref[shelf.back] = back_matrix(rows + rest, height)
    lane = lax.broadcasted_iota(jnp.int32, (len(rows) * SUB, cols), 1)
    fetch_clear.wait()
    turn_flags(clear_held, flags_in, flags)

    for step in range(dates // SUB):
        at = pl.ds(step * SUB, SUB)
        here = pl.ds(step * SUB * height, SUB * height)
        clear = flags[at, :]
        lines = flag_lines(clear, repeat, own)
        cover = product(lines, columns).astype(jnp.bfloat16)
        shelf_ref[here, :] = cover
        for q, ref in ((0, first_ref), (height - 1, last_ref)):
            kept = jnp.where(lax.div(flag_lane, blocks) == q, clear.astype(jnp.float32), 0.0)
            ref[flat, at, :] = kept.astype(jnp.bfloat16)
        shelf_ref[shelf.near[step]] = product(turn_rest, lines).astype(jnp.bfloat16)
        count = product(product(turn, lines).astype(jnp.bfloat16), box)
        scale = 1.0 / jnp.maximum(count, 1.0)
        fetch(step).wait()
        for b in range(bands):
            masked = held_ref[b, here, :] * cover
            masked_ref[b, here, :] = masked
            ends = product(edges, masked).astype(jnp.bfloat16)
            for i, ref in enumerate((first_ref, last_ref)):
                for k in range(blocks):
                    ref[b * blocks + k, at, :] = ends[i * SUB : (i + 1) * SUB, k * LANES : (k + 1) * LANES]
            file_lines(table, at, smooth_lines(product(turn, masked), scale, lane), rows, b, bands)
    give_pieces(table, pieces)


def smooth_first(refl, clear, chunks, chips):
    bands, lines, cols = refl.shape
    height, blocks, dates = clear.shape
    number = bands * blocks * len(chunks[0])
    width = padded(height * blocks)
    pieces = [jax.ShapeDtypeStruct((number // chips, dates, LANES), jnp.bfloat16)] * chips
    size = Shelf(chunks[1], height, blocks, dates).size
    held = [pltpu.VMEM((bands + 1, size, cols), jnp.bfloat16)]
    edges = [jax.ShapeDtypeStruct((bands * blocks + 1, dates, width), jnp.bfloat16)] * 2
    return pl.pallas_call(
        functools.partial(first_kernel, chunks, chips),
        in_specs=[pl.BlockSpec(memory_space=pltpu.HBM)] * 2,
        out_specs=[pl.BlockSpec(memory_space=pltpu.VMEM)] * (chips + 3),
        out_shape=pieces + held + edges,
        scratch_shapes=[
            pltpu.VMEM((number, dates, LANES), jnp.bfloat16),
            pltpu.VMEM(refl.shape, refl.dtype),
            pltpu.VMEM(clear.shape, clear.dtype),
            pltpu.VMEM((width, padded(dates)), jnp.float32),
            pltpu.VMEM((padded(dates), width), jnp.bfloat16),
            pltpu.SemaphoreType.DMA((dates // SUB + 1,)),
        ],
        compiler_params=pltpu.CompilerParams(vmem_limit_bytes=14 * MIB),
        name="smooth_first",
    )(pltpu.with_memory_space_constraint(refl, pltpu.HBM), pltpu.with_memory_space_constraint(clear, pltpu.HBM))


def rest_kernel(rows, chips, height, masked_ref, before_ref, after_ref, *refs):
    pieces, table = refs[:chips], refs[chips]
    bands, cols = masked_ref.shape[0] - 1, masked_ref.shape[2]
    dates = pieces[0].shape[1]
    blocks = cols // LANES
    flat = bands * blocks
    shelf_ref = masked_ref.at[bands]
    shelf = Shelf(rows, height, blocks, dates)
    halo = tuple((rows.index(q), ref) for q, ref in ((0, before_ref), (height - 1, after_ref)))
    box, turn = shelf_ref[shelf.box], shelf_ref[shelf.turn]
    lane = lax.broadcasted_iota(jnp.int32, (len(rows) * SUB, cols), 1)
    for step in range(dates // SUB):
        at = pl.ds(step * SUB, SUB)
        here = pl.ds(step * SUB * height, SUB * height)
        count = product(shelf_ref[shelf.near[step]], box)
        for place, ref in halo:
            count = add_row(count, place, product(ref[flat, at, :], box))
        scale = 1.0 / jnp.maximum(count, 1.0)
        for b in range(bands):
            down = product(turn, masked_ref[b, here, :])
            for place, ref in halo:
                extra = jnp.concatenate([ref[b * blocks + k, at, :] for k in range(blocks)], axis=1)
                down = add_row(down, place, extra.astype(jnp.float32))
            file_lines(table, at, smooth_lines(down, scale, lane), rows, b, bands)
    give_pieces(table, pieces)


def hand_on_kernel(first_in, last_in, first_out, last_out):
    first_out[...] = first_in[...]
    last_out[...] = last_in[...]


def hand_on(first, last):
    return pl.pallas_call(
        hand_on_kernel,
        out_shape=[jax.ShapeDtypeStruct(x.shape, x.dtype) for x in (first, last)],
        compiler_params=pltpu.CompilerParams(vmem_limit_bytes=8 * MIB),
        name="hand_on",
    )(first, last)


def smooth_rest(masked, height, halo, rows, chips):
    bands, cols = masked.shape[0] - 1, masked.shape[2]
    dates = halo[0].shape[1]
    number = bands * (cols // LANES) * len(rows)
    return pl.pallas_call(
        functools.partial(rest_kernel, rows, chips, height),
        in_specs=[pl.BlockSpec(memory_space=pltpu.VMEM)] * 3,
        out_shape=[jax.ShapeDtypeStruct((number // chips, dates, LANES), jnp.bfloat16)] * chips,
        scratch_shapes=[pltpu.VMEM((number, dates, LANES), jnp.bfloat16)],
        compiler_params=pltpu.CompilerParams(vmem_limit_bytes=12 * MIB),
        name="smooth_rest",
    )(masked, *halo)


def filter_kernel(dates, wave_ref, high_ref, low_ref):
    total = high_ref.shape[1]
    chips = total // dates // 2
    core = lax.axis_index(DATE) % 2
    wave = jnp.concatenate(
        [jnp.broadcast_to(wave_ref[a : a + 1, :], (dates, LANES)) for a in range(total // LANES)], axis=1
    )
    same = pltpu.roll(wave, 0, 1, stride=1, stride_axis=0)
    other = jnp.where(core == 0, pltpu.roll(same, total - dates, 1), pltpu.roll(same, dates, 1))
    for side, base in enumerate((same, other)):
        high = base.astype(jnp.bfloat16)
        low = (base - high.astype(jnp.float32)).astype(jnp.bfloat16)
        for ref, part in ((high_ref, high), (low_ref, low)):
            for q in range(chips):
                for s in range(chips):
                    at = (s - q) % chips * 2 * dates
                    left = (side * chips + s) * dates
                    ref[q * dates : (q + 1) * dates, left : left + dates] = part[:, at : at + dates]


def filter_matrix(harmonics, dates, peers):
    total = dates * peers
    fine = jnp.arange(LANES, dtype=jnp.int32)
    coarse = jnp.arange(0, total, LANES, dtype=jnp.int32)

    def turned(steps):
        angle = (harmonics[:, None] * steps[None, :] % total).astype(jnp.float32) * (2.0 * math.pi / total)
        return jnp.cos(angle), jnp.sin(angle)

    (cos_a, sin_a), (cos_b, sin_b) = turned(coarse), turned(fine)
    wave = jnp.einsum(
        "fa,fb->ab",
        jnp.concatenate([cos_a, sin_a], axis=0),
        jnp.concatenate([cos_b, -sin_b], axis=0),
        precision=lax.Precision.HIGHEST,
    )
    wave = wave * (2.0 / total)
    return pl.pallas_call(
        functools.partial(filter_kernel, dates),
        out_shape=[jax.ShapeDtypeStruct((total // 2, total), jnp.bfloat16)] * 2,
        compiler_params=pltpu.CompilerParams(vmem_limit_bytes=10 * MIB),
        name="filter_matrix",
    )(wave)


def pack_kernel(chips, *refs):
    pieces, out_ref = refs[:chips], refs[-1]
    units, dates, lanes = pieces[0].shape
    chip = lax.axis_index(DATE) // 2
    for m in range(chips):
        at = pl.multiple_of((chip ^ m) * dates, dates)
        for i in range(units):
            part = (pl.ds(at, dates), pl.ds(i * lanes, lanes))
            for side in ((0,), (1,)) if len(out_ref.shape) == 3 else ((),):
                out_ref[side + part] = pieces[m][i]


def pack(pieces, after, copies):
    units, dates, lanes = pieces[0].shape
    shape = (len(pieces) * dates, units * lanes)
    return pl.pallas_call(
        functools.partial(pack_kernel, len(pieces)),
        in_specs=[pl.BlockSpec(memory_space=pltpu.VMEM)] * len(pieces)
        + [pl.BlockSpec(memory_space=pl.ANY)] * len(after),
        out_shape=jax.ShapeDtypeStruct((copies, *shape) if copies > 1 else shape, jnp.bfloat16),
        compiler_params=pltpu.CompilerParams(vmem_limit_bytes=8 * MIB),
        name="pack",
    )(*pieces, *after)


def apply_kernel(chips, shared, high_ref, low_ref, *refs):
    outs, result = refs[-2] if shared else refs[-1 - chips : -1], refs[-1]
    units, dates, lanes = outs.shape[1:] if shared else outs[0].shape
    half = high_ref.shape[0]
    chip, core = lax.axis_index(DATE) // 2, lax.axis_index(DATE) % 2
    own_ref, other_ref = (refs[0].at[core], refs[0].at[1 - core]) if shared else refs[:2]
    tile = min(half, 256)

    @pl.loop(0, half // tile)
    def _(step):
        at = pl.ds(pl.multiple_of(step * tile, tile), tile)
        total = None
        for ref in (high_ref, low_ref):
            for series, left in ((own_ref, 0), (other_ref, half)):
                part = product(ref[at, left : left + half], series[...])
                total = part if total is None else total + part
        result[at, :] = total

    for m in range(chips):
        at = m * dates if shared else pl.multiple_of((chip ^ m) * dates, dates)
        out = outs.at[m] if shared else outs[m]
        for i in range(units):
            out[i] = result[pl.ds(at, dates), i * lanes : (i + 1) * lanes].astype(jnp.bfloat16)


def apply_filter(high, low, series, chips):
    half, width = series[0].shape[-2:]
    piece = jax.ShapeDtypeStruct((width // LANES, half // chips, LANES), jnp.bfloat16)
    shared = len(series) == 1
    return pl.pallas_call(
        functools.partial(apply_kernel, chips, shared),
        out_shape=jax.ShapeDtypeStruct((chips, *piece.shape), piece.dtype) if shared else [piece] * chips,
        scratch_shapes=[pltpu.VMEM((half, width), jnp.float32)],
        compiler_params=pltpu.CompilerParams(vmem_limit_bytes=16 * MIB),
        name="apply_filter",
    )(high, low, *series)


def anomaly_kernel(chunks, chips, masked_ref, *refs):
    pieces, whole_ref, (out_ref, table, held, turn_held, made, sems) = refs[:chips], refs[chips], refs[chips + 1 :]
    bands, lines, cols = made.shape
    dates = table.shape[1]
    height = lines // dates
    blocks = cols // LANES
    chip = lax.axis_index(DATE) // 2
    turn_at, turn_cols = Shelf(chunks[1], height, blocks, dates).back
    fetch_turn = pltpu.make_async_copy(masked_ref.at[bands, turn_at], turn_held, sems.at[0, bands + 1])

    def fetch(step):
        here = pl.ds(step * SUB * height, SUB * height)
        return pltpu.make_async_copy(masked_ref.at[:, here], held.at[:, here], sems.at[step, bands])

    fetch_turn.start()
    for step in range(dates // SUB):
        fetch(step).start()
    order, start = [], 0
    for c, rows in enumerate(chunks):
        units = whole_ref.shape[1] if c > 0 else pieces[0].shape[0]
        for m in range(chips):
            if c > 0:
                table[pl.ds(start + m * units, units)] = whole_ref[m]
            else:
                table[pl.ds(start + (chip ^ m) * units, units)] = pieces[m][...]
        order += [(r, start + i * bands, len(rows) * bands) for i, r in enumerate(rows)]
        start += units * chips

    fetch_turn.wait()
    turn = turn_held[:, turn_cols]

    def store(step, b):
        here = pl.ds(step * SUB * height, SUB * height)
        return pltpu.make_async_copy(made.at[b, here], out_ref.at[b, here], sems.at[step, b])

    for step in range(dates // SUB):
        at = pl.ds(step * SUB, SUB)
        here = pl.ds(step * SUB * height, SUB * height)
        fetch(step).wait()
        cover = held[bands, here, :].astype(jnp.float32)
        for b in range(bands):
            seasonal = jnp.concatenate(
                [
                    jnp.concatenate([table[first + k * step_k + b, at, :] for k in range(blocks)], axis=1)
                    for _, first, step_k in order
                ],
                axis=0,
            )
            made[b, here, :] = held[b, here, :].astype(jnp.float32) - cover * product(turn, seasonal)
            store(step, b).start()
    for step in range(dates // SUB):
        for b in range(bands):
            store(step, b).wait()


def anomaly(masked, height, chunks, pieces, chips):
    bands, cols = masked.shape[0] - 1, masked.shape[2]
    dates = pieces[0].shape[1]
    lines = dates * height
    return pl.pallas_call(
        functools.partial(anomaly_kernel, chunks, chips),
        in_specs=[pl.BlockSpec(memory_space=pltpu.HBM)] + [pl.BlockSpec(memory_space=pltpu.VMEM)] * len(pieces),
        out_specs=pl.BlockSpec(memory_space=pl.ANY),
        out_shape=jax.ShapeDtypeStruct((bands, lines, cols), jnp.float32),
        scratch_shapes=[
            pltpu.VMEM((bands * cols // LANES * height, dates, LANES), jnp.bfloat16),
            pltpu.VMEM((bands + 1, lines, cols), jnp.bfloat16),
            pltpu.VMEM((SUB * height, cols), jnp.bfloat16),
            pltpu.VMEM((bands, lines, cols), jnp.float32),
            pltpu.SemaphoreType.DMA((dates // SUB, bands + 2)),
        ],
        compiler_params=pltpu.CompilerParams(vmem_limit_bytes=20 * MIB),
        name="anomaly",
    )(pltpu.with_memory_space_constraint(masked, pltpu.HBM), *pieces)


def exchange(pieces, peers):
    out = list(pieces)
    for m in range(len(pieces) - 1, 0, -1):
        out[m] = lax.ppermute(pieces[m], DATE, [(i, i ^ (2 * m)) for i in range(peers)])
    return out


def on_device(reflectance, clear_sky, harmonics):
    bands, dates, height, cols = reflectance.shape
    peers, tiles = lax.axis_size(DATE), lax.axis_size(TILE)
    chips = peers // 2
    clear = jnp.transpose(clear_sky, (1, 2, 0))
    chunks = (tuple(range(1, height - 1)), (height - 1, 0))
    refl = reflectance.reshape(bands, dates * height, cols)
    out = smooth_first(refl, clear, chunks, chips)
    masked, first, last = out[chips:]
    inner = exchange(out[:chips], peers)
    first, last = hand_on(first, last)
    up = [(i, i + 1) for i in range(tiles - 1)]
    before = lax.ppermute(last, TILE, up)
    after = lax.ppermute(first, TILE, [(j, i) for i, j in up])
    edges = smooth_rest(masked, height, (before, after), chunks[1], chips)
    outer = exchange(edges, peers)
    high, low = filter_matrix(harmonics, dates, peers)
    own = pack(inner, (high, edges[0]), 1)
    other = lax.ppermute(own, DATE, [(i, i ^ 1) for i in range(peers)])
    made = apply_filter(high, low, (own, other), chips)
    results = exchange(made, peers)
    own = pack(outer, (made[0],), 2)
    both = lax.all_to_all(own, DATE, 0, 0, axis_index_groups=[[i, i + 1] for i in range(0, peers, 2)])
    made = apply_filter(high, low, (both,), chips)
    cores = [list(range(core, peers, 2)) for core in range(2)]
    results.append(lax.all_to_all(made, DATE, 0, 0, axis_index_groups=cores))
    return anomaly(masked, height, chunks, results, chips).reshape(reflectance.shape)


def solution(mesh):
    return jax.shard_map(
        on_device,
        mesh=mesh,
        in_specs=(P(None, DATE, TILE, None), P(DATE, TILE, None), P()),
        out_specs=P(None, DATE, TILE, None),
        check_vma=False,
    )
```

```python
import functools
import math

import jax
import jax.numpy as jnp
from jax import lax
from jax.experimental import pallas as pl
from jax.experimental.pallas import tpu as pltpu
from jax.sharding import PartitionSpec as P

LANES = 128
SUB = 32
MIB = 2**20
CLOUD = 1e30
DATE, TILE = ("date", "tile")


def apart(m, chips, core):
    bits = (chips - m) % chips
    width = chips.bit_length() - 1
    return sum((bits >> k & 1) << (width - 1 - k) for k in range(width)) if core else bits


def partner(m, chips):
    me = lax.axis_index(DATE)
    return (me // 2) ^ jnp.where(me % 2 == 0, apart(m, chips, 0), apart(m, chips, 1))


def padded(size):
    return -(-size // LANES) * LANES


def turn_flags(clear_ref, flags_in, flags):
    height, blocks, dates = clear_ref.shape
    flags_in[...] = jnp.zeros_like(flags_in)
    for q in range(height):
        flags_in[q * blocks : (q + 1) * blocks, 0:dates] = clear_ref[q].astype(jnp.float32)
    flags[...] = flags_in[...].T.astype(jnp.bfloat16)


def grid_of(shape):
    return lax.broadcasted_iota(jnp.int32, shape, 0), lax.broadcasted_iota(jnp.int32, shape, 1)


def table_of(index, values):
    out = jnp.zeros_like(index)
    for i, value in enumerate(values):
        out = jnp.where(index == i, value, out)
    return out


def as_matrix(choice):
    return jnp.where(choice, 1.0, 0.0).astype(jnp.bfloat16)


def product(left, right):
    return jnp.dot(left, right, preferred_element_type=jnp.float32)


def add_row(lines, place, extra):
    parts = [lines[i : i + SUB] for i in range(0, lines.shape[0], SUB)]
    parts[place] = parts[place] + extra
    return jnp.concatenate(parts, axis=0)


def cover_matrices(height, blocks, width):
    line, date = grid_of((SUB * height, SUB))
    repeat = as_matrix(lax.div(line, height) == date)
    line, lane = grid_of((SUB * height, width))
    own = lax.rem(line, height) == lax.div(lane, blocks)
    lane, column = grid_of((width, blocks * LANES))
    columns = as_matrix(lax.rem(lane, blocks) == lax.div(column, LANES))
    return repeat, own, columns


def box_columns(blocks, width):
    lane, column = grid_of((width, blocks * LANES))
    total = jnp.zeros(lane.shape, jnp.float32)
    for shift in (-1, 0, 1):
        at = column + shift
        there = jnp.where(at < 0, -1, lax.div(at, LANES))
        total = total + jnp.where(there == lax.rem(lane, blocks), 1.0, 0.0)
    return total.astype(jnp.bfloat16)


def flag_lines(clear, repeat, own):
    return jnp.where(own, product(repeat, clear), 0.0).astype(jnp.bfloat16)


def turn_matrix(rows, height):
    line, source = grid_of((len(rows) * SUB, SUB * height))
    apart = jnp.abs(table_of(lax.div(line, SUB), rows) - lax.rem(source, height))
    return as_matrix((lax.rem(line, SUB) == lax.div(source, height)) & (apart <= 1))


def back_matrix(rows, height):
    line, source = grid_of((SUB * height, len(rows) * SUB))
    row = table_of(lax.div(source, SUB), rows)
    return as_matrix((lax.div(line, height) == lax.rem(source, SUB)) & (lax.rem(line, height) == row))


class Shelf:
    def __init__(self, rows, height, blocks, dates):
        width = padded(height * blocks)
        lines = len(rows) * SUB
        start = dates * height
        self.box = (pl.ds(start, width), pl.ds(0, blocks * LANES))
        start += width
        self.near = [(pl.ds(start + step * lines, lines), pl.ds(0, width)) for step in range(dates // SUB)]
        self.turn = (pl.ds(start, lines), pl.ds(width, SUB * height))
        self.size = start + dates // SUB * lines


def smooth_lines(down, scale, lane):
    cols = down.shape[1]
    west = jnp.where(lane == 0, 0.0, pltpu.roll(down, 1, 1))
    east = jnp.where(lane == cols - 1, 0.0, pltpu.roll(down, cols - 1, 1))
    return ((down + west + east) * scale).astype(jnp.bfloat16)


def file_lines(table, at, smoothed, rows, b, bands):
    blocks = smoothed.shape[1] // LANES
    for k in range(blocks):
        for i in range(len(rows)):
            part = smoothed[i * SUB : (i + 1) * SUB, k * LANES : (k + 1) * LANES]
            table[(k * len(rows) + i) * bands + b, at, :] = part


def give_pieces(table, pieces):
    units = table.shape[0] // len(pieces)
    for m, piece in enumerate(pieces):
        piece[...] = table[pl.ds(partner(m, len(pieces)) * units, units)]


def first_kernel(chunks, chips, refl_ref, clear_ref, *refs):
    pieces, refs = refs[:chips], refs[chips:]
    masked_ref, first_ref, last_ref = refs[:3]
    table, held_ref, clear_held, flags_in, flags, sems = refs[3:]
    rows, rest = chunks
    bands, lines_all, cols = refl_ref.shape
    dates = pieces[0].shape[1]
    height = lines_all // dates
    shelf_ref = masked_ref.at[bands]
    blocks = cols // LANES
    flat = bands * blocks
    width = flags.shape[1]
    shelf = Shelf(rest, height, blocks, dates)

    def fetch(step):
        at = pl.ds(step * SUB * height, SUB * height)
        return pltpu.make_async_copy(refl_ref.at[:, at], held_ref.at[:, at], sems.at[step])

    fetch_clear = pltpu.make_async_copy(clear_ref, clear_held, sems.at[dates // SUB])
    fetch_clear.start()
    for step in range(dates // SUB):
        fetch(step).start()
    line, source = grid_of((2 * SUB, SUB * height))
    edge = jnp.where(line < SUB, 0, height - 1)
    edges = as_matrix((lax.rem(line, SUB) == lax.div(source, height)) & (edge == lax.rem(source, height)))
    flag_lane = lax.broadcasted_iota(jnp.int32, (SUB, width), 1)
    repeat, own, columns = cover_matrices(height, blocks, width)
    box = box_columns(blocks, width)
    turn = turn_matrix(rows, height)
    turn_rest = turn_matrix(rest, height)
    shelf_ref[shelf.box] = box
    shelf_ref[shelf.turn] = turn_rest
    lane = lax.broadcasted_iota(jnp.int32, (len(rows) * SUB, cols), 1)
    fetch_clear.wait()
    turn_flags(clear_held, flags_in, flags)

    for step in range(dates // SUB):
        at = pl.ds(step * SUB, SUB)
        here = pl.ds(step * SUB * height, SUB * height)
        clear = flags[at, :]
        lines = flag_lines(clear, repeat, own)
        cover = product(lines, columns).astype(jnp.bfloat16)
        shelf_ref[here, :] = cover
        for q, ref in ((0, first_ref), (height - 1, last_ref)):
            kept = jnp.where(lax.div(flag_lane, blocks) == q, clear.astype(jnp.float32), 0.0)
            ref[flat, at, :] = kept.astype(jnp.bfloat16)
        shelf_ref[shelf.near[step]] = product(turn_rest, lines).astype(jnp.bfloat16)
        count = product(product(turn, lines).astype(jnp.bfloat16), box)
        scale = 1.0 / jnp.maximum(count, 1.0)
        cloud = CLOUD - CLOUD * cover
        fetch(step).wait()
        for b in range(bands):
            masked = held_ref[b, here, :] * cover
            masked_ref[b, here, :] = masked + cloud
            ends = product(edges, masked).astype(jnp.bfloat16)
            for i, ref in enumerate((first_ref, last_ref)):
                for k in range(blocks):
                    ref[b * blocks + k, at, :] = ends[i * SUB : (i + 1) * SUB, k * LANES : (k + 1) * LANES]
            file_lines(table, at, smooth_lines(product(turn, masked), scale, lane), rows, b, bands)
    give_pieces(table, pieces)


def smooth_first(refl, clear, chunks, chips):
    bands, lines, cols = refl.shape
    height, blocks, dates = clear.shape
    number = bands * blocks * len(chunks[0])
    width = padded(height * blocks)
    pieces = [jax.ShapeDtypeStruct((number // chips, dates, LANES), jnp.bfloat16)] * chips
    size = Shelf(chunks[1], height, blocks, dates).size
    held = [pltpu.VMEM((bands + 1, size, cols), jnp.bfloat16)]
    edges = [jax.ShapeDtypeStruct((bands * blocks + 1, dates, width), jnp.bfloat16)] * 2
    return pl.pallas_call(
        functools.partial(first_kernel, chunks, chips),
        in_specs=[pl.BlockSpec(memory_space=pltpu.HBM)] * 2,
        out_specs=[pl.BlockSpec(memory_space=pltpu.VMEM)] * (chips + 3),
        out_shape=pieces + held + edges,
        scratch_shapes=[
            pltpu.VMEM((number, dates, LANES), jnp.bfloat16),
            pltpu.VMEM(refl.shape, refl.dtype),
            pltpu.VMEM(clear.shape, clear.dtype),
            pltpu.VMEM((width, padded(dates)), jnp.float32),
            pltpu.VMEM((padded(dates), width), jnp.bfloat16),
            pltpu.SemaphoreType.DMA((dates // SUB + 1,)),
        ],
        compiler_params=pltpu.CompilerParams(vmem_limit_bytes=14 * MIB),
        name="smooth_first",
    )(pltpu.with_memory_space_constraint(refl, pltpu.HBM), pltpu.with_memory_space_constraint(clear, pltpu.HBM))


def rest_kernel(rows, chips, height, masked_ref, before_ref, after_ref, *refs):
    pieces, table = refs[:chips], refs[chips]
    bands, cols = masked_ref.shape[0] - 1, masked_ref.shape[2]
    dates = pieces[0].shape[1]
    blocks = cols // LANES
    flat = bands * blocks
    shelf_ref = masked_ref.at[bands]
    shelf = Shelf(rows, height, blocks, dates)
    halo = tuple((rows.index(q), ref) for q, ref in ((0, before_ref), (height - 1, after_ref)))
    box, turn = shelf_ref[shelf.box], shelf_ref[shelf.turn]
    lane = lax.broadcasted_iota(jnp.int32, (len(rows) * SUB, cols), 1)
    for step in range(dates // SUB):
        at = pl.ds(step * SUB, SUB)
        here = pl.ds(step * SUB * height, SUB * height)
        count = product(shelf_ref[shelf.near[step]], box)
        for place, ref in halo:
            count = add_row(count, place, product(ref[flat, at, :], box))
        scale = 1.0 / jnp.maximum(count, 1.0)
        for b in range(bands):
            down = product(turn, masked_ref[b, here, :] * shelf_ref[here, :])
            for place, ref in halo:
                extra = jnp.concatenate([ref[b * blocks + k, at, :] for k in range(blocks)], axis=1)
                down = add_row(down, place, extra.astype(jnp.float32))
            file_lines(table, at, smooth_lines(down, scale, lane), rows, b, bands)
    give_pieces(table, pieces)


def hand_on_kernel(first_in, last_in, first_out, last_out):
    first_out[...] = first_in[...]
    last_out[...] = last_in[...]


def hand_on(first, last):
    return pl.pallas_call(
        hand_on_kernel,
        out_shape=[jax.ShapeDtypeStruct(x.shape, x.dtype) for x in (first, last)],
        compiler_params=pltpu.CompilerParams(vmem_limit_bytes=8 * MIB),
        name="hand_on",
    )(first, last)


def smooth_rest(masked, height, halo, rows, chips):
    bands, cols = masked.shape[0] - 1, masked.shape[2]
    dates = halo[0].shape[1]
    number = bands * (cols // LANES) * len(rows)
    return pl.pallas_call(
        functools.partial(rest_kernel, rows, chips, height),
        in_specs=[pl.BlockSpec(memory_space=pltpu.VMEM)] * 3,
        out_shape=[jax.ShapeDtypeStruct((number // chips, dates, LANES), jnp.bfloat16)] * chips,
        scratch_shapes=[pltpu.VMEM((number, dates, LANES), jnp.bfloat16)],
        compiler_params=pltpu.CompilerParams(vmem_limit_bytes=12 * MIB),
        name="smooth_rest",
    )(masked, *halo)


def filter_kernel(dates, wave_ref, high_ref, low_ref):
    total = high_ref.shape[1]
    chips = total // dates // 2
    core = lax.axis_index(DATE) % 2
    wave = jnp.concatenate(
        [jnp.broadcast_to(wave_ref[a : a + 1, :], (dates, LANES)) for a in range(total // LANES)], axis=1
    )
    same = pltpu.roll(wave, 0, 1, stride=1, stride_axis=0)
    other = jnp.where(core == 0, pltpu.roll(same, total - dates, 1), pltpu.roll(same, dates, 1))
    for side, base in enumerate((same, other)):
        high = base.astype(jnp.bfloat16)
        low = (base - high.astype(jnp.float32)).astype(jnp.bfloat16)
        for ref, part in ((high_ref, high), (low_ref, low)):
            for q in range(chips):
                for s in range(chips):
                    at = (s - q) % chips * 2 * dates
                    left = (side * chips + s) * dates
                    ref[q * dates : (q + 1) * dates, left : left + dates] = part[:, at : at + dates]


def filter_matrix(harmonics, dates, peers):
    total = dates * peers
    fine = jnp.arange(LANES, dtype=jnp.int32)
    coarse = jnp.arange(0, total, LANES, dtype=jnp.int32)

    def turned(steps):
        angle = (harmonics[:, None] * steps[None, :] % total).astype(jnp.float32) * (2.0 * math.pi / total)
        return jnp.cos(angle), jnp.sin(angle)

    (cos_a, sin_a), (cos_b, sin_b) = turned(coarse), turned(fine)
    wave = jnp.einsum(
        "fa,fb->ab",
        jnp.concatenate([cos_a, sin_a], axis=0),
        jnp.concatenate([cos_b, -sin_b], axis=0),
        precision=lax.Precision.HIGHEST,
    )
    wave = wave * (2.0 / total)
    return pl.pallas_call(
        functools.partial(filter_kernel, dates),
        out_shape=[jax.ShapeDtypeStruct((total // 2, total), jnp.bfloat16)] * 2,
        compiler_params=pltpu.CompilerParams(vmem_limit_bytes=10 * MIB),
        name="filter_matrix",
    )(wave)


def pack_kernel(chips, *refs):
    pieces, out_ref = refs[:chips], refs[-1]
    units, dates, lanes = pieces[0].shape
    chip = lax.axis_index(DATE) // 2
    for m in range(chips):
        at = pl.multiple_of(partner(m, chips) * dates, dates)
        for i in range(units):
            part = (pl.ds(at, dates), pl.ds(i * lanes, lanes))
            for side in ((0,), (1,)) if len(out_ref.shape) == 3 else ((),):
                out_ref[side + part] = pieces[m][i]


def pack(pieces, after, copies):
    units, dates, lanes = pieces[0].shape
    shape = (len(pieces) * dates, units * lanes)
    return pl.pallas_call(
        functools.partial(pack_kernel, len(pieces)),
        in_specs=[pl.BlockSpec(memory_space=pltpu.VMEM)] * len(pieces)
        + [pl.BlockSpec(memory_space=pl.ANY)] * len(after),
        out_shape=jax.ShapeDtypeStruct((copies, *shape) if copies > 1 else shape, jnp.bfloat16),
        compiler_params=pltpu.CompilerParams(vmem_limit_bytes=8 * MIB),
        name="pack",
    )(*pieces, *after)


def apply_kernel(chips, shared, high_ref, low_ref, *refs):
    outs, result = refs[-2] if shared else refs[-1 - chips : -1], refs[-1]
    units, dates, lanes = outs.shape[1:] if shared else outs[0].shape
    half = high_ref.shape[0]
    chip, core = lax.axis_index(DATE) // 2, lax.axis_index(DATE) % 2
    own_ref, other_ref = (refs[0].at[core], refs[0].at[1 - core]) if shared else refs[:2]
    tile = min(half, 256)

    @pl.loop(0, half // tile)
    def _(step):
        at = pl.ds(pl.multiple_of(step * tile, tile), tile)
        total = None
        for ref in (high_ref, low_ref):
            for series, left in ((own_ref, 0), (other_ref, half)):
                part = product(ref[at, left : left + half], series[...])
                total = part if total is None else total + part
        result[at, :] = total

    for m in range(chips):
        at = m * dates if shared else pl.multiple_of(partner(m, chips) * dates, dates)
        out = outs.at[m] if shared else outs[m]
        for i in range(units):
            out[i] = result[pl.ds(at, dates), i * lanes : (i + 1) * lanes].astype(jnp.bfloat16)


def apply_filter(high, low, series, chips):
    half, width = series[0].shape[-2:]
    piece = jax.ShapeDtypeStruct((width // LANES, half // chips, LANES), jnp.bfloat16)
    shared = len(series) == 1
    return pl.pallas_call(
        functools.partial(apply_kernel, chips, shared),
        out_shape=jax.ShapeDtypeStruct((chips, *piece.shape), piece.dtype) if shared else [piece] * chips,
        scratch_shapes=[pltpu.VMEM((half, width), jnp.float32)],
        compiler_params=pltpu.CompilerParams(vmem_limit_bytes=16 * MIB),
        name="apply_filter",
    )(high, low, *series)


def anomaly_kernel(chunks, chips, masked_ref, *refs):
    pieces, whole_ref, (out_ref, table, held, made, sems) = refs[:chips], refs[chips], refs[chips + 1 :]
    bands, lines, cols = made.shape
    dates = table.shape[1]
    height = lines // dates
    blocks = cols // LANES
    chip = lax.axis_index(DATE) // 2
    def fetch(step):
        here = pl.ds(step * SUB * height, SUB * height)
        return pltpu.make_async_copy(masked_ref.at[0:bands, here], held.at[:, here], sems.at[step, bands])

    for step in range(dates // SUB):
        fetch(step).start()
    turn = back_matrix(chunks[0] + chunks[1], height)
    order, start = [], 0
    for c, rows in enumerate(chunks):
        units = whole_ref.shape[1] if c > 0 else pieces[0].shape[0]
        for m in range(chips):
            if c > 0:
                table[pl.ds(start + m * units, units)] = whole_ref[m]
            else:
                table[pl.ds(start + partner(m, chips) * units, units)] = pieces[m][...]
        order += [(start + i * bands, len(rows) * bands) for i in range(len(rows))]
        start += units * chips

    def store(step, b):
        here = pl.ds(step * SUB * height, SUB * height)
        return pltpu.make_async_copy(made.at[b, here], out_ref.at[b, here], sems.at[step, b])

    for step in range(dates // SUB):
        at = pl.ds(step * SUB, SUB)
        here = pl.ds(step * SUB * height, SUB * height)
        fetch(step).wait()
        for b in range(bands):
            seasonal = jnp.concatenate(
                [
                    jnp.concatenate([table[first + k * step_k + b, at, :] for k in range(blocks)], axis=1)
                    for first, step_k in order
                ],
                axis=0,
            )
            clear = held[b, here, :].astype(jnp.float32)
            made[b, here, :] = jnp.where(clear < CLOUD / 2, clear - product(turn, seasonal), 0.0)
            store(step, b).start()
    for step in range(dates // SUB):
        for b in range(bands):
            store(step, b).wait()


def anomaly(masked, height, chunks, pieces, chips):
    bands, cols = masked.shape[0] - 1, masked.shape[2]
    dates = pieces[0].shape[1]
    lines = dates * height
    return pl.pallas_call(
        functools.partial(anomaly_kernel, chunks, chips),
        in_specs=[pl.BlockSpec(memory_space=pltpu.HBM)] + [pl.BlockSpec(memory_space=pltpu.VMEM)] * len(pieces),
        out_specs=pl.BlockSpec(memory_space=pl.ANY),
        out_shape=jax.ShapeDtypeStruct((bands, lines, cols), jnp.float32),
        scratch_shapes=[
            pltpu.VMEM((bands * cols // LANES * height, dates, LANES), jnp.bfloat16),
            pltpu.VMEM((bands, lines, cols), jnp.bfloat16),
            pltpu.VMEM((bands, lines, cols), jnp.float32),
            pltpu.SemaphoreType.DMA((dates // SUB, bands + 1)),
        ],
        compiler_params=pltpu.CompilerParams(vmem_limit_bytes=20 * MIB),
        name="anomaly",
    )(pltpu.with_memory_space_constraint(masked, pltpu.HBM), *pieces)


def exchange(pieces, peers):
    out = list(pieces)
    for m in range(len(pieces) - 1, 0, -1):
        to = [(i, i ^ (2 * apart(m, len(pieces), i % 2))) for i in range(peers)]
        out[m] = lax.ppermute(pieces[m], DATE, to)
    return out


def on_device(reflectance, clear_sky, harmonics):
    bands, dates, height, cols = reflectance.shape
    peers, tiles = lax.axis_size(DATE), lax.axis_size(TILE)
    chips = peers // 2
    clear = jnp.transpose(clear_sky, (1, 2, 0))
    chunks = (tuple(range(1, height - 1)), (height - 1, 0))
    refl = reflectance.reshape(bands, dates * height, cols)
    out = smooth_first(refl, clear, chunks, chips)
    masked, first, last = out[chips:]
    inner = exchange(out[:chips], peers)
    first, last = hand_on(first, last)
    up = [(i, i + 1) for i in range(tiles - 1)]
    before = lax.ppermute(last, TILE, up)
    after = lax.ppermute(first, TILE, [(j, i) for i, j in up])
    edges = smooth_rest(masked, height, (before, after), chunks[1], chips)
    outer = exchange(edges, peers)
    high, low = filter_matrix(harmonics, dates, peers)
    own = pack(inner, (high, edges[0]), 1)
    other = lax.ppermute(own, DATE, [(i, i ^ 1) for i in range(peers)])
    made = apply_filter(high, low, (own, other), chips)
    results = exchange(made, peers)
    own = pack(outer, (made[0],), 2)
    both = lax.all_to_all(own, DATE, 0, 0, axis_index_groups=[[i, i + 1] for i in range(0, peers, 2)])
    made = apply_filter(high, low, (both,), chips)
    cores = [list(range(core, peers, 2)) for core in range(2)]
    results.append(lax.all_to_all(made, DATE, 0, 0, axis_index_groups=cores))
    return anomaly(masked, height, chunks, results, chips).reshape(reflectance.shape)


def solution(mesh):
    return jax.shard_map(
        on_device,
        mesh=mesh,
        in_specs=(P(None, DATE, TILE, None), P(DATE, TILE, None), P()),
        out_specs=P(None, DATE, TILE, None),
        check_vma=False,
    )
```

```python
import functools
import math

import jax
import jax.numpy as jnp
from jax import lax
from jax.experimental import pallas as pl
from jax.experimental.pallas import tpu as pltpu
from jax.sharding import PartitionSpec as P

LANES = 128
SUB = 32
MIB = 2**20
CLOUD = 1e30
DATE, TILE = ("date", "tile")


def apart(m, chips, core):
    bits = (chips - m) % chips
    width = chips.bit_length() - 1
    return sum((bits >> k & 1) << (width - 1 - k) for k in range(width)) if core else bits


def partner(m, chips):
    me = lax.axis_index(DATE)
    return (me // 2) ^ jnp.where(me % 2 == 0, apart(m, chips, 0), apart(m, chips, 1))


def padded(size):
    return -(-size // LANES) * LANES


def turn_flags(clear_ref, flags_in, flags):
    height, blocks, dates = clear_ref.shape
    flags_in[...] = jnp.zeros_like(flags_in)
    for q in range(height):
        flags_in[q * blocks : (q + 1) * blocks, 0:dates] = clear_ref[q].astype(jnp.float32)
    flags[...] = flags_in[...].T.astype(jnp.bfloat16)


def grid_of(shape):
    return lax.broadcasted_iota(jnp.int32, shape, 0), lax.broadcasted_iota(jnp.int32, shape, 1)


def table_of(index, values):
    out = jnp.zeros_like(index)
    for i, value in enumerate(values):
        out = jnp.where(index == i, value, out)
    return out


def as_matrix(choice):
    return jnp.where(choice, 1.0, 0.0).astype(jnp.bfloat16)


def product(left, right):
    return jnp.dot(left, right, preferred_element_type=jnp.float32)


def add_row(lines, place, extra):
    parts = [lines[i : i + SUB] for i in range(0, lines.shape[0], SUB)]
    parts[place] = parts[place] + extra
    return jnp.concatenate(parts, axis=0)


def cover_matrices(height, blocks, width):
    line, date = grid_of((SUB * height, SUB))
    repeat = as_matrix(lax.div(line, height) == date)
    line, lane = grid_of((SUB * height, width))
    own = lax.rem(line, height) == lax.div(lane, blocks)
    lane, column = grid_of((width, blocks * LANES))
    columns = as_matrix(lax.rem(lane, blocks) == lax.div(column, LANES))
    return repeat, own, columns


def box_columns(blocks, width):
    lane, column = grid_of((width, blocks * LANES))
    total = jnp.zeros(lane.shape, jnp.float32)
    for shift in (-1, 0, 1):
        at = column + shift
        there = jnp.where(at < 0, -1, lax.div(at, LANES))
        total = total + jnp.where(there == lax.rem(lane, blocks), 1.0, 0.0)
    return total.astype(jnp.bfloat16)


def flag_lines(clear, repeat, own):
    return jnp.where(own, product(repeat, clear), 0.0).astype(jnp.bfloat16)


def turn_matrix(rows, height):
    line, source = grid_of((len(rows) * SUB, SUB * height))
    apart = jnp.abs(table_of(lax.div(line, SUB), rows) - lax.rem(source, height))
    return as_matrix((lax.rem(line, SUB) == lax.div(source, height)) & (apart <= 1))


def back_matrix(rows, height):
    line, source = grid_of((SUB * height, len(rows) * SUB))
    row = table_of(lax.div(source, SUB), rows)
    return as_matrix((lax.div(line, height) == lax.rem(source, SUB)) & (lax.rem(line, height) == row))


class Shelf:
    def __init__(self, rows, height, blocks, dates):
        width = padded(height * blocks)
        lines = len(rows) * SUB
        start = dates * height
        self.box = (pl.ds(start, width), pl.ds(0, blocks * LANES))
        start += width
        self.near = [(pl.ds(start + step * lines, lines), pl.ds(0, width)) for step in range(dates // SUB)]
        self.turn = (pl.ds(start, lines), pl.ds(width, SUB * height))
        self.size = start + dates // SUB * lines


def smooth_lines(down, scale, lane):
    cols = down.shape[1]
    west = jnp.where(lane == 0, 0.0, pltpu.roll(down, 1, 1))
    east = jnp.where(lane == cols - 1, 0.0, pltpu.roll(down, cols - 1, 1))
    return ((down + west + east) * scale).astype(jnp.bfloat16)


def file_lines(table, at, smoothed, rows, b, bands):
    blocks = smoothed.shape[1] // LANES
    for k in range(blocks):
        for i in range(len(rows)):
            part = smoothed[i * SUB : (i + 1) * SUB, k * LANES : (k + 1) * LANES]
            table[(k * len(rows) + i) * bands + b, at, :] = part


def give_pieces(table, pieces):
    units = table.shape[0] // len(pieces)
    for m, piece in enumerate(pieces):
        piece[...] = table[pl.ds(partner(m, len(pieces)) * units, units)]


def first_kernel(chunks, chips, refl_ref, clear_ref, *refs):
    pieces, refs = refs[:chips], refs[chips:]
    masked_ref, first_ref, last_ref = refs[:3]
    table, held_ref, clear_held, flags_in, flags, sems = refs[3:]
    rows, rest = chunks
    bands, lines_all, cols = refl_ref.shape
    dates = pieces[0].shape[1]
    height = lines_all // dates
    shelf_ref = masked_ref.at[bands]
    blocks = cols // LANES
    flat = bands * blocks
    width = flags.shape[1]
    shelf = Shelf(rest, height, blocks, dates)

    def fetch(step):
        at = pl.ds(step * SUB * height, SUB * height)
        return pltpu.make_async_copy(refl_ref.at[:, at], held_ref.at[:, at], sems.at[step])

    fetch_clear = pltpu.make_async_copy(clear_ref, clear_held, sems.at[dates // SUB])
    fetch_clear.start()
    for step in range(dates // SUB):
        fetch(step).start()
    line, source = grid_of((2 * SUB, SUB * height))
    edge = jnp.where(line < SUB, 0, height - 1)
    edges = as_matrix((lax.rem(line, SUB) == lax.div(source, height)) & (edge == lax.rem(source, height)))
    flag_lane = lax.broadcasted_iota(jnp.int32, (SUB, width), 1)
    repeat, own, columns = cover_matrices(height, blocks, width)
    box = box_columns(blocks, width)
    turn = turn_matrix(rows, height)
    turn_rest = turn_matrix(rest, height)
    shelf_ref[shelf.box] = box
    shelf_ref[shelf.turn] = turn_rest
    lane = lax.broadcasted_iota(jnp.int32, (len(rows) * SUB, cols), 1)
    fetch_clear.wait()
    turn_flags(clear_held, flags_in, flags)

    for step in range(dates // SUB):
        at = pl.ds(step * SUB, SUB)
        here = pl.ds(step * SUB * height, SUB * height)
        clear = flags[at, :]
        lines = flag_lines(clear, repeat, own)
        cover = product(lines, columns).astype(jnp.bfloat16)
        shelf_ref[here, :] = cover
        for q, ref in ((0, first_ref), (height - 1, last_ref)):
            kept = jnp.where(lax.div(flag_lane, blocks) == q, clear.astype(jnp.float32), 0.0)
            ref[flat, at, :] = kept.astype(jnp.bfloat16)
        shelf_ref[shelf.near[step]] = product(turn_rest, lines).astype(jnp.bfloat16)
        count = product(product(turn, lines).astype(jnp.bfloat16), box)
        scale = 1.0 / jnp.maximum(count, 1.0)
        cloud = CLOUD - CLOUD * cover
        fetch(step).wait()
        for b in range(bands):
            masked = held_ref[b, here, :] * cover
            masked_ref[b, here, :] = masked + cloud
            ends = product(edges, masked).astype(jnp.bfloat16)
            for i, ref in enumerate((first_ref, last_ref)):
                for k in range(blocks):
                    ref[b * blocks + k, at, :] = ends[i * SUB : (i + 1) * SUB, k * LANES : (k + 1) * LANES]
            file_lines(table, at, smooth_lines(product(turn, masked), scale, lane), rows, b, bands)
    give_pieces(table, pieces)


def smooth_first(refl, clear, chunks, chips):
    bands, lines, cols = refl.shape
    height, blocks, dates = clear.shape
    number = bands * blocks * len(chunks[0])
    width = padded(height * blocks)
    pieces = [jax.ShapeDtypeStruct((number // chips, dates, LANES), jnp.bfloat16)] * chips
    size = Shelf(chunks[1], height, blocks, dates).size
    held = [pltpu.VMEM((bands + 1, size, cols), jnp.bfloat16)]
    edges = [jax.ShapeDtypeStruct((bands * blocks + 1, dates, width), jnp.bfloat16)] * 2
    return pl.pallas_call(
        functools.partial(first_kernel, chunks, chips),
        in_specs=[pl.BlockSpec(memory_space=pltpu.HBM)] * 2,
        out_specs=[pl.BlockSpec(memory_space=pltpu.VMEM)] * (chips + 3),
        out_shape=pieces + held + edges,
        scratch_shapes=[
            pltpu.VMEM((number, dates, LANES), jnp.bfloat16),
            pltpu.VMEM(refl.shape, refl.dtype),
            pltpu.VMEM(clear.shape, clear.dtype),
            pltpu.VMEM((width, padded(dates)), jnp.float32),
            pltpu.VMEM((padded(dates), width), jnp.bfloat16),
            pltpu.SemaphoreType.DMA((dates // SUB + 1,)),
        ],
        compiler_params=pltpu.CompilerParams(vmem_limit_bytes=14 * MIB),
        name="smooth_first",
    )(pltpu.with_memory_space_constraint(refl, pltpu.HBM), pltpu.with_memory_space_constraint(clear, pltpu.HBM))


def rest_kernel(rows, chips, height, masked_ref, before_ref, after_ref, *refs):
    pieces, table = refs[:chips], refs[chips]
    bands, cols = masked_ref.shape[0] - 1, masked_ref.shape[2]
    dates = pieces[0].shape[1]
    blocks = cols // LANES
    flat = bands * blocks
    shelf_ref = masked_ref.at[bands]
    shelf = Shelf(rows, height, blocks, dates)
    halo = tuple((rows.index(q), ref) for q, ref in ((0, before_ref), (height - 1, after_ref)))
    box, turn = shelf_ref[shelf.box], shelf_ref[shelf.turn]
    lane = lax.broadcasted_iota(jnp.int32, (len(rows) * SUB, cols), 1)
    for step in range(dates // SUB):
        at = pl.ds(step * SUB, SUB)
        here = pl.ds(step * SUB * height, SUB * height)
        count = product(shelf_ref[shelf.near[step]], box)
        for place, ref in halo:
            count = add_row(count, place, product(ref[flat, at, :], box))
        scale = 1.0 / jnp.maximum(count, 1.0)
        for b in range(bands):
            down = product(turn, masked_ref[b, here, :] * shelf_ref[here, :])
            for place, ref in halo:
                extra = jnp.concatenate([ref[b * blocks + k, at, :] for k in range(blocks)], axis=1)
                down = add_row(down, place, extra.astype(jnp.float32))
            file_lines(table, at, smooth_lines(down, scale, lane), rows, b, bands)
    give_pieces(table, pieces)


def hand_on_kernel(first_in, last_in, first_out, last_out):
    first_out[...] = first_in[...]
    last_out[...] = last_in[...]


def hand_on(first, last):
    return pl.pallas_call(
        hand_on_kernel,
        out_shape=[jax.ShapeDtypeStruct(x.shape, x.dtype) for x in (first, last)],
        compiler_params=pltpu.CompilerParams(vmem_limit_bytes=8 * MIB),
        name="hand_on",
    )(first, last)


def smooth_rest(masked, height, halo, rows, chips):
    bands, cols = masked.shape[0] - 1, masked.shape[2]
    dates = halo[0].shape[1]
    number = bands * (cols // LANES) * len(rows)
    return pl.pallas_call(
        functools.partial(rest_kernel, rows, chips, height),
        in_specs=[pl.BlockSpec(memory_space=pltpu.VMEM)] * 3,
        out_shape=[jax.ShapeDtypeStruct((number // chips, dates, LANES), jnp.bfloat16)] * chips,
        scratch_shapes=[pltpu.VMEM((number, dates, LANES), jnp.bfloat16)],
        compiler_params=pltpu.CompilerParams(vmem_limit_bytes=12 * MIB),
        name="smooth_rest",
    )(masked, *halo)


def filter_kernel(dates, wave_ref, high_ref, low_ref):
    total = high_ref.shape[1]
    chips = total // dates // 2
    core = lax.axis_index(DATE) % 2
    wave = jnp.concatenate(
        [jnp.broadcast_to(wave_ref[a : a + 1, :], (dates, LANES)) for a in range(total // LANES)], axis=1
    )
    same = pltpu.roll(wave, 0, 1, stride=1, stride_axis=0)
    other = jnp.where(core == 0, pltpu.roll(same, total - dates, 1), pltpu.roll(same, dates, 1))
    for side, base in enumerate((same, other)):
        high = base.astype(jnp.bfloat16)
        low = (base - high.astype(jnp.float32)).astype(jnp.bfloat16)
        for ref, part in ((high_ref, high), (low_ref, low)):
            for q in range(chips):
                for s in range(chips):
                    at = (s - q) % chips * 2 * dates
                    left = (side * chips + s) * dates
                    ref[q * dates : (q + 1) * dates, left : left + dates] = part[:, at : at + dates]


def filter_matrix(harmonics, dates, peers):
    total = dates * peers
    fine = jnp.arange(LANES, dtype=jnp.int32)
    coarse = jnp.arange(0, total, LANES, dtype=jnp.int32)

    def turned(steps):
        angle = (harmonics[:, None] * steps[None, :] % total).astype(jnp.float32) * (2.0 * math.pi / total)
        return jnp.cos(angle), jnp.sin(angle)

    (cos_a, sin_a), (cos_b, sin_b) = turned(coarse), turned(fine)
    wave = jnp.einsum(
        "fa,fb->ab",
        jnp.concatenate([cos_a, sin_a], axis=0),
        jnp.concatenate([cos_b, -sin_b], axis=0),
        precision=lax.Precision.HIGHEST,
    )
    wave = wave * (2.0 / total)
    return pl.pallas_call(
        functools.partial(filter_kernel, dates),
        out_shape=[jax.ShapeDtypeStruct((total // 2, total), jnp.bfloat16)] * 2,
        compiler_params=pltpu.CompilerParams(vmem_limit_bytes=10 * MIB),
        name="filter_matrix",
    )(wave)


def pack_kernel(chips, *refs):
    pieces, out_ref = refs[:chips], refs[-1]
    units, dates, lanes = pieces[0].shape
    chip = lax.axis_index(DATE) // 2
    for m in range(chips):
        at = pl.multiple_of(partner(m, chips) * dates, dates)
        for i in range(units):
            part = (pl.ds(at, dates), pl.ds(i * lanes, lanes))
            for side in ((0,), (1,)) if len(out_ref.shape) == 3 else ((),):
                out_ref[side + part] = pieces[m][i]


def pack(pieces, after, copies):
    units, dates, lanes = pieces[0].shape
    shape = (len(pieces) * dates, units * lanes)
    return pl.pallas_call(
        functools.partial(pack_kernel, len(pieces)),
        in_specs=[pl.BlockSpec(memory_space=pltpu.VMEM)] * len(pieces)
        + [pl.BlockSpec(memory_space=pl.ANY)] * len(after),
        out_shape=jax.ShapeDtypeStruct((copies, *shape) if copies > 1 else shape, jnp.bfloat16),
        compiler_params=pltpu.CompilerParams(vmem_limit_bytes=8 * MIB),
        name="pack",
    )(*pieces, *after)


def apply_kernel(chips, shared, high_ref, low_ref, *refs):
    outs = refs[-1] if shared else refs[-chips:]
    units, dates, lanes = outs.shape[1:] if shared else outs[0].shape
    half = high_ref.shape[0]
    core = lax.axis_index(DATE) % 2
    own_ref, other_ref = (refs[0].at[core], refs[0].at[1 - core]) if shared else refs[:2]
    for m in range(chips):
        at = pl.ds(m * dates if shared else pl.multiple_of(partner(m, chips) * dates, dates), dates)
        out = outs.at[m] if shared else outs[m]
        total = None
        for ref in (high_ref, low_ref):
            for series, left in ((own_ref, 0), (other_ref, half)):
                part = product(ref[at, left : left + half], series[...])
                total = part if total is None else total + part
        for i in range(units):
            out[i] = total[:, i * lanes : (i + 1) * lanes].astype(jnp.bfloat16)


def apply_filter(high, low, series, chips):
    half, width = series[0].shape[-2:]
    piece = jax.ShapeDtypeStruct((width // LANES, half // chips, LANES), jnp.bfloat16)
    shared = len(series) == 1
    return pl.pallas_call(
        functools.partial(apply_kernel, chips, shared),
        out_shape=jax.ShapeDtypeStruct((chips, *piece.shape), piece.dtype) if shared else [piece] * chips,
        compiler_params=pltpu.CompilerParams(vmem_limit_bytes=16 * MIB),
        name="apply_filter",
    )(high, low, *series)


def anomaly_kernel(chunks, chips, masked_ref, *refs):
    pieces, whole_ref, (out_ref, table, held, made, sems) = refs[:chips], refs[chips], refs[chips + 1 :]
    bands, lines, cols = made.shape
    dates = table.shape[1]
    height = lines // dates
    blocks = cols // LANES
    chip = lax.axis_index(DATE) // 2
    def fetch(step):
        here = pl.ds(step * SUB * height, SUB * height)
        return pltpu.make_async_copy(masked_ref.at[0:bands, here], held.at[:, here], sems.at[step, bands])

    for step in range(dates // SUB):
        fetch(step).start()
    turn = back_matrix(chunks[0] + chunks[1], height)
    order, start = [], 0
    for c, rows in enumerate(chunks):
        units = whole_ref.shape[1] if c > 0 else pieces[0].shape[0]
        for m in range(chips):
            if c > 0:
                table[pl.ds(start + m * units, units)] = whole_ref[m]
            else:
                table[pl.ds(start + partner(m, chips) * units, units)] = pieces[m][...]
        order += [(start + i * bands, len(rows) * bands) for i in range(len(rows))]
        start += units * chips

    def store(step, b):
        here = pl.ds(step * SUB * height, SUB * height)
        return pltpu.make_async_copy(made.at[b, here], out_ref.at[b, here], sems.at[step, b])

    for step in range(dates // SUB):
        at = pl.ds(step * SUB, SUB)
        here = pl.ds(step * SUB * height, SUB * height)
        fetch(step).wait()
        for b in range(bands):
            seasonal = jnp.concatenate(
                [
                    jnp.concatenate([table[first + k * step_k + b, at, :] for k in range(blocks)], axis=1)
                    for first, step_k in order
                ],
                axis=0,
            )
            clear = held[b, here, :].astype(jnp.float32)
            made[b, here, :] = jnp.where(clear < CLOUD / 2, clear - product(turn, seasonal), 0.0)
            store(step, b).start()
    for step in range(dates // SUB):
        for b in range(bands):
            store(step, b).wait()


def anomaly(masked, height, chunks, pieces, chips):
    bands, cols = masked.shape[0] - 1, masked.shape[2]
    dates = pieces[0].shape[1]
    lines = dates * height
    return pl.pallas_call(
        functools.partial(anomaly_kernel, chunks, chips),
        in_specs=[pl.BlockSpec(memory_space=pltpu.HBM)] + [pl.BlockSpec(memory_space=pltpu.VMEM)] * len(pieces),
        out_specs=pl.BlockSpec(memory_space=pl.ANY),
        out_shape=jax.ShapeDtypeStruct((bands, lines, cols), jnp.float32),
        scratch_shapes=[
            pltpu.VMEM((bands * cols // LANES * height, dates, LANES), jnp.bfloat16),
            pltpu.VMEM((bands, lines, cols), jnp.bfloat16),
            pltpu.VMEM((bands, lines, cols), jnp.float32),
            pltpu.SemaphoreType.DMA((dates // SUB, bands + 1)),
        ],
        compiler_params=pltpu.CompilerParams(vmem_limit_bytes=20 * MIB),
        name="anomaly",
    )(pltpu.with_memory_space_constraint(masked, pltpu.HBM), *pieces)


def exchange(pieces, peers):
    out = list(pieces)
    for m in range(len(pieces) - 1, 0, -1):
        to = [(i, i ^ (2 * apart(m, len(pieces), i % 2))) for i in range(peers)]
        out[m] = lax.ppermute(pieces[m], DATE, to)
    return out


def on_device(reflectance, clear_sky, harmonics):
    bands, dates, height, cols = reflectance.shape
    peers, tiles = lax.axis_size(DATE), lax.axis_size(TILE)
    chips = peers // 2
    clear = jnp.transpose(clear_sky, (1, 2, 0))
    chunks = (tuple(range(1, height - 1)), (height - 1, 0))
    refl = reflectance.reshape(bands, dates * height, cols)
    out = smooth_first(refl, clear, chunks, chips)
    masked, first, last = out[chips:]
    inner = exchange(out[:chips], peers)
    first, last = hand_on(first, last)
    up = [(i, i + 1) for i in range(tiles - 1)]
    before = lax.ppermute(last, TILE, up)
    after = lax.ppermute(first, TILE, [(j, i) for i, j in up])
    edges = smooth_rest(masked, height, (before, after), chunks[1], chips)
    outer = exchange(edges, peers)
    high, low = filter_matrix(harmonics, dates, peers)
    own = pack(inner, (high, edges[0]), 1)
    other = lax.ppermute(own, DATE, [(i, i ^ 1) for i in range(peers)])
    made = apply_filter(high, low, (own, other), chips)
    results = exchange(made, peers)
    own = pack(outer, (made[0],), 2)
    both = lax.all_to_all(own, DATE, 0, 0, axis_index_groups=[[i, i + 1] for i in range(0, peers, 2)])
    made = apply_filter(high, low, (both,), chips)
    cores = [list(range(core, peers, 2)) for core in range(2)]
    results.append(lax.all_to_all(made, DATE, 0, 0, axis_index_groups=cores))
    return anomaly(masked, height, chunks, results, chips).reshape(reflectance.shape)


def solution(mesh):
    return jax.shard_map(
        on_device,
        mesh=mesh,
        in_specs=(P(None, DATE, TILE, None), P(DATE, TILE, None), P()),
        out_specs=P(None, DATE, TILE, None),
        check_vma=False,
    )
```

```python
import functools
import math

import jax
import jax.numpy as jnp
from jax import lax
from jax.experimental import pallas as pl
from jax.experimental.pallas import tpu as pltpu
from jax.sharding import PartitionSpec as P

LANES = 128
SUB = 32
MIB = 2**20
CLOUD = 1e30
DATE, TILE = ("date", "tile")


def apart(m, chips, core):
    bits = (chips - m) % chips
    width = chips.bit_length() - 1
    return sum((bits >> k & 1) << (width - 1 - k) for k in range(width)) if core else bits


def partner(m, chips, side=0):
    me = lax.axis_index(DATE)
    return (me // 2) ^ jnp.where(me % 2 == side, apart(m, chips, 0), apart(m, chips, 1))


def padded(size):
    return -(-size // LANES) * LANES


def turn_flags(clear_ref, flags_in, flags):
    height, blocks, dates = clear_ref.shape
    flags_in[...] = jnp.zeros_like(flags_in)
    for q in range(height):
        flags_in[q * blocks : (q + 1) * blocks, 0:dates] = clear_ref[q].astype(jnp.float32)
    flags[...] = flags_in[...].T.astype(jnp.bfloat16)


def grid_of(shape):
    return lax.broadcasted_iota(jnp.int32, shape, 0), lax.broadcasted_iota(jnp.int32, shape, 1)


def table_of(index, values):
    out = jnp.zeros_like(index)
    for i, value in enumerate(values):
        out = jnp.where(index == i, value, out)
    return out


def as_matrix(choice):
    return jnp.where(choice, 1.0, 0.0).astype(jnp.bfloat16)


def product(left, right):
    return jnp.dot(left, right, preferred_element_type=jnp.float32)


def add_row(lines, place, extra):
    parts = [lines[i : i + SUB] for i in range(0, lines.shape[0], SUB)]
    parts[place] = parts[place] + extra
    return jnp.concatenate(parts, axis=0)


def cover_matrices(height, blocks, width):
    line, date = grid_of((SUB * height, SUB))
    repeat = as_matrix(lax.div(line, height) == date)
    line, lane = grid_of((SUB * height, width))
    own = lax.rem(line, height) == lax.div(lane, blocks)
    lane, column = grid_of((width, blocks * LANES))
    columns = as_matrix(lax.rem(lane, blocks) == lax.div(column, LANES))
    return repeat, own, columns


def box_columns(blocks, width):
    lane, column = grid_of((width, blocks * LANES))
    total = jnp.zeros(lane.shape, jnp.float32)
    for shift in (-1, 0, 1):
        at = column + shift
        there = jnp.where(at < 0, -1, lax.div(at, LANES))
        total = total + jnp.where(there == lax.rem(lane, blocks), 1.0, 0.0)
    return total.astype(jnp.bfloat16)


def flag_lines(clear, repeat, own):
    return jnp.where(own, product(repeat, clear), 0.0).astype(jnp.bfloat16)


def turn_matrix(rows, height):
    line, source = grid_of((len(rows) * SUB, SUB * height))
    apart = jnp.abs(table_of(lax.div(line, SUB), rows) - lax.rem(source, height))
    return as_matrix((lax.rem(line, SUB) == lax.div(source, height)) & (apart <= 1))


def back_matrix(rows, height):
    line, source = grid_of((SUB * height, len(rows) * SUB))
    row = table_of(lax.div(source, SUB), rows)
    return as_matrix((lax.div(line, height) == lax.rem(source, SUB)) & (lax.rem(line, height) == row))


class Shelf:
    def __init__(self, rows, height, blocks, dates):
        width = padded(height * blocks)
        lines = len(rows) * SUB
        start = dates * height
        self.box = (pl.ds(start, width), pl.ds(0, blocks * LANES))
        start += width
        self.near = [(pl.ds(start + step * lines, lines), pl.ds(0, width)) for step in range(dates // SUB)]
        self.turn = (pl.ds(start, lines), pl.ds(width, SUB * height))
        self.size = start + dates // SUB * lines


def smooth_lines(down, scale, lane):
    cols = down.shape[1]
    west = jnp.where(lane == 0, 0.0, pltpu.roll(down, 1, 1))
    east = jnp.where(lane == cols - 1, 0.0, pltpu.roll(down, cols - 1, 1))
    return ((down + west + east) * scale).astype(jnp.bfloat16)


def file_lines(table, at, smoothed, rows, b, bands):
    blocks = smoothed.shape[1] // LANES
    for k in range(blocks):
        for i in range(len(rows)):
            part = smoothed[i * SUB : (i + 1) * SUB, k * LANES : (k + 1) * LANES]
            table[(k * len(rows) + i) * bands + b, at, :] = part


def give_pieces(table, pieces):
    units = table.shape[0] // len(pieces)
    for m, piece in enumerate(pieces):
        piece[...] = table[pl.ds(partner(m, len(pieces)) * units, units)]


def first_kernel(chunks, chips, refl_ref, clear_ref, *refs):
    pieces, refs = refs[:chips], refs[chips:]
    masked_ref, first_ref, last_ref = refs[:3]
    table, held_ref, clear_held, flags_in, flags, sems = refs[3:]
    rows, rest = chunks
    bands, lines_all, cols = refl_ref.shape
    dates = pieces[0].shape[1]
    height = lines_all // dates
    shelf_ref = masked_ref.at[bands]
    blocks = cols // LANES
    flat = bands * blocks
    width = flags.shape[1]
    shelf = Shelf(rest, height, blocks, dates)

    def fetch(step):
        at = pl.ds(step * SUB * height, SUB * height)
        return pltpu.make_async_copy(refl_ref.at[:, at], held_ref.at[:, at], sems.at[step])

    fetch_clear = pltpu.make_async_copy(clear_ref, clear_held, sems.at[dates // SUB])
    fetch_clear.start()
    for step in range(dates // SUB):
        fetch(step).start()
    line, source = grid_of((2 * SUB, SUB * height))
    edge = jnp.where(line < SUB, 0, height - 1)
    edges = as_matrix((lax.rem(line, SUB) == lax.div(source, height)) & (edge == lax.rem(source, height)))
    flag_lane = lax.broadcasted_iota(jnp.int32, (SUB, width), 1)
    repeat, own, columns = cover_matrices(height, blocks, width)
    box = box_columns(blocks, width)
    turn = turn_matrix(rows, height)
    turn_rest = turn_matrix(rest, height)
    shelf_ref[shelf.box] = box
    shelf_ref[shelf.turn] = turn_rest
    lane = lax.broadcasted_iota(jnp.int32, (len(rows) * SUB, cols), 1)
    fetch_clear.wait()
    turn_flags(clear_held, flags_in, flags)

    for step in range(dates // SUB):
        at = pl.ds(step * SUB, SUB)
        here = pl.ds(step * SUB * height, SUB * height)
        clear = flags[at, :]
        lines = flag_lines(clear, repeat, own)
        cover = product(lines, columns).astype(jnp.bfloat16)
        shelf_ref[here, :] = cover
        for q, ref in ((0, first_ref), (height - 1, last_ref)):
            kept = jnp.where(lax.div(flag_lane, blocks) == q, clear.astype(jnp.float32), 0.0)
            ref[flat, at, :] = kept.astype(jnp.bfloat16)
        shelf_ref[shelf.near[step]] = product(turn_rest, lines).astype(jnp.bfloat16)
        count = product(product(turn, lines).astype(jnp.bfloat16), box)
        scale = 1.0 / jnp.maximum(count, 1.0)
        cloud = CLOUD - CLOUD * cover
        fetch(step).wait()
        for b in range(bands):
            masked = held_ref[b, here, :] * cover
            masked_ref[b, here, :] = masked + cloud
            ends = product(edges, masked).astype(jnp.bfloat16)
            for i, ref in enumerate((first_ref, last_ref)):
                for k in range(blocks):
                    ref[b * blocks + k, at, :] = ends[i * SUB : (i + 1) * SUB, k * LANES : (k + 1) * LANES]
            file_lines(table, at, smooth_lines(product(turn, masked), scale, lane), rows, b, bands)
    give_pieces(table, pieces)


def smooth_first(refl, clear, chunks, chips):
    bands, lines, cols = refl.shape
    height, blocks, dates = clear.shape
    number = bands * blocks * len(chunks[0])
    width = padded(height * blocks)
    pieces = [jax.ShapeDtypeStruct((number // chips, dates, LANES), jnp.bfloat16)] * chips
    size = Shelf(chunks[1], height, blocks, dates).size
    held = [pltpu.VMEM((bands + 1, size, cols), jnp.bfloat16)]
    edges = [jax.ShapeDtypeStruct((bands * blocks + 1, dates, width), jnp.bfloat16)] * 2
    return pl.pallas_call(
        functools.partial(first_kernel, chunks, chips),
        in_specs=[pl.BlockSpec(memory_space=pltpu.HBM)] * 2,
        out_specs=[pl.BlockSpec(memory_space=pltpu.VMEM)] * (chips + 3),
        out_shape=pieces + held + edges,
        scratch_shapes=[
            pltpu.VMEM((number, dates, LANES), jnp.bfloat16),
            pltpu.VMEM(refl.shape, refl.dtype),
            pltpu.VMEM(clear.shape, clear.dtype),
            pltpu.VMEM((width, padded(dates)), jnp.float32),
            pltpu.VMEM((padded(dates), width), jnp.bfloat16),
            pltpu.SemaphoreType.DMA((dates // SUB + 1,)),
        ],
        compiler_params=pltpu.CompilerParams(vmem_limit_bytes=14 * MIB),
        name="smooth_first",
    )(pltpu.with_memory_space_constraint(refl, pltpu.HBM), pltpu.with_memory_space_constraint(clear, pltpu.HBM))


def rest_kernel(rows, chips, height, masked_ref, before_ref, after_ref, *refs):
    pieces, table = refs[:chips], refs[chips]
    bands, cols = masked_ref.shape[0] - 1, masked_ref.shape[2]
    dates = pieces[0].shape[1]
    blocks = cols // LANES
    flat = bands * blocks
    shelf_ref = masked_ref.at[bands]
    shelf = Shelf(rows, height, blocks, dates)
    halo = tuple((rows.index(q), ref) for q, ref in ((0, before_ref), (height - 1, after_ref)))
    box, turn = shelf_ref[shelf.box], shelf_ref[shelf.turn]
    lane = lax.broadcasted_iota(jnp.int32, (len(rows) * SUB, cols), 1)
    for step in range(dates // SUB):
        at = pl.ds(step * SUB, SUB)
        here = pl.ds(step * SUB * height, SUB * height)
        count = product(shelf_ref[shelf.near[step]], box)
        for place, ref in halo:
            count = add_row(count, place, product(ref[flat, at, :], box))
        scale = 1.0 / jnp.maximum(count, 1.0)
        for b in range(bands):
            down = product(turn, masked_ref[b, here, :] * shelf_ref[here, :])
            for place, ref in halo:
                extra = jnp.concatenate([ref[b * blocks + k, at, :] for k in range(blocks)], axis=1)
                down = add_row(down, place, extra.astype(jnp.float32))
            file_lines(table, at, smooth_lines(down, scale, lane), rows, b, bands)
    give_pieces(table, pieces)


def hand_on_kernel(first_in, last_in, first_out, last_out):
    first_out[...] = first_in[...]
    last_out[...] = last_in[...]


def hand_on(first, last):
    return pl.pallas_call(
        hand_on_kernel,
        out_shape=[jax.ShapeDtypeStruct(x.shape, x.dtype) for x in (first, last)],
        compiler_params=pltpu.CompilerParams(vmem_limit_bytes=8 * MIB),
        name="hand_on",
    )(first, last)


def smooth_rest(masked, height, halo, rows, chips):
    bands, cols = masked.shape[0] - 1, masked.shape[2]
    dates = halo[0].shape[1]
    number = bands * (cols // LANES) * len(rows)
    return pl.pallas_call(
        functools.partial(rest_kernel, rows, chips, height),
        in_specs=[pl.BlockSpec(memory_space=pltpu.VMEM)] * 3,
        out_shape=[jax.ShapeDtypeStruct((number // chips, dates, LANES), jnp.bfloat16)] * chips,
        scratch_shapes=[pltpu.VMEM((number, dates, LANES), jnp.bfloat16)],
        compiler_params=pltpu.CompilerParams(vmem_limit_bytes=12 * MIB),
        name="smooth_rest",
    )(masked, *halo)


def filter_kernel(dates, wave_ref, high_ref, low_ref, turned):
    total = high_ref.shape[1]
    chips = total // dates // 2
    core = lax.axis_index(DATE) % 2
    wave = jnp.concatenate(
        [jnp.broadcast_to(wave_ref[a : a + 1, :], (dates, LANES)) for a in range(total // LANES)], axis=1
    )
    same = pltpu.roll(wave, 0, 1, stride=1, stride_axis=0)
    other = jnp.where(core == 0, pltpu.roll(same, total - dates, 1), pltpu.roll(same, dates, 1))
    for side, base in enumerate((same, other)):
        high = base.astype(jnp.bfloat16)
        low = (base - high.astype(jnp.float32)).astype(jnp.bfloat16)
        for n, (ref, part) in enumerate(((high_ref, high), (low_ref, low))):
            turned[2 * side + n] = part
            for m in range(chips):
                for q in range(chips):
                    step = lax.rem(partner(m, chips, side) + chips - q, chips)
                    at = pl.multiple_of(step * 2 * dates, LANES)
                    left = (side * chips + m) * dates
                    ref[q * dates : (q + 1) * dates, left : left + dates] = turned[2 * side + n, :, pl.ds(at, dates)]


def filter_matrix(harmonics, dates, peers):
    total = dates * peers
    fine = jnp.arange(LANES, dtype=jnp.int32)
    coarse = jnp.arange(0, total, LANES, dtype=jnp.int32)

    def turned(steps):
        angle = (harmonics[:, None] * steps[None, :] % total).astype(jnp.float32) * (2.0 * math.pi / total)
        return jnp.cos(angle), jnp.sin(angle)

    (cos_a, sin_a), (cos_b, sin_b) = turned(coarse), turned(fine)
    wave = jnp.einsum(
        "fa,fb->ab",
        jnp.concatenate([cos_a, sin_a], axis=0),
        jnp.concatenate([cos_b, -sin_b], axis=0),
        precision=lax.Precision.HIGHEST,
    )
    wave = wave * (2.0 / total)
    return pl.pallas_call(
        functools.partial(filter_kernel, dates),
        out_shape=[jax.ShapeDtypeStruct((total // 2, total), jnp.bfloat16)] * 2,
        scratch_shapes=[pltpu.VMEM((4, dates, total), jnp.bfloat16)],
        compiler_params=pltpu.CompilerParams(vmem_limit_bytes=10 * MIB),
        name="filter_matrix",
    )(wave)


def pack_kernel(chips, *refs):
    pieces, out_ref = refs[:chips], refs[-1]
    units, dates, lanes = pieces[0].shape
    for m in range(chips):
        at = m * dates
        for i in range(units):
            part = (pl.ds(at, dates), pl.ds(i * lanes, lanes))
            for side in ((0,), (1,)) if len(out_ref.shape) == 3 else ((),):
                out_ref[side + part] = pieces[m][i]


def pack(pieces, after, copies):
    units, dates, lanes = pieces[0].shape
    shape = (len(pieces) * dates, units * lanes)
    return pl.pallas_call(
        functools.partial(pack_kernel, len(pieces)),
        in_specs=[pl.BlockSpec(memory_space=pltpu.VMEM)] * len(pieces)
        + [pl.BlockSpec(memory_space=pl.ANY)] * len(after),
        out_shape=jax.ShapeDtypeStruct((copies, *shape) if copies > 1 else shape, jnp.bfloat16),
        compiler_params=pltpu.CompilerParams(vmem_limit_bytes=8 * MIB),
        name="pack",
    )(*pieces, *after)


def begin_kernel(high_ref, low_ref, *refs):
    pieces, (result, series) = refs[:-2], refs[-2:]
    units, dates, lanes = pieces[0].shape
    for m, piece in enumerate(pieces):
        for i in range(units):
            series[m * dates : (m + 1) * dates, i * lanes : (i + 1) * lanes] = piece[i]
    depth, tile = series.shape[0], dates
    for at in range(0, result.shape[0], tile):
        lines = pl.ds(at, tile)
        result[lines, :] = product(high_ref[lines, :depth], series[...]) + product(low_ref[lines, :depth], series[...])


def begin(high, low, pieces):
    units, dates, lanes = pieces[0].shape
    return pl.pallas_call(
        begin_kernel,
        out_shape=jax.ShapeDtypeStruct((high.shape[0], units * lanes), jnp.float32),
        scratch_shapes=[pltpu.VMEM((len(pieces) * dates, units * lanes), jnp.bfloat16)],
        compiler_params=pltpu.CompilerParams(vmem_limit_bytes=12 * MIB),
        name="begin",
    )(high, low, *pieces)


def apply_kernel(chips, shared, done, high_ref, low_ref, *refs):
    outs = refs[-1] if shared else refs[-chips:]
    units, dates, lanes = outs.shape[1:] if shared else outs[0].shape
    half = high_ref.shape[0]
    core = lax.axis_index(DATE) % 2
    own_ref, other_ref = (refs[0].at[core], refs[0].at[1 - core]) if shared else refs[:2]
    begun = done * dates
    for m in range(chips):
        at = pl.ds(m * dates if shared else pl.multiple_of(partner(m, chips) * dates, dates), dates)
        out = outs.at[m] if shared else outs[m]
        total = refs[2][at, :] if done > 0 else None
        for ref in (high_ref, low_ref):
            for series, first, left in ((own_ref, begun, 0), (other_ref, 0, half)):
                part = product(ref[at, left + first : left + half], series[first:half, :])
                total = part if total is None else total + part
        for i in range(units):
            out[i] = total[:, i * lanes : (i + 1) * lanes].astype(jnp.bfloat16)


def apply_filter(high, low, series, chips, begun=(), done=0):
    half, width = series[0].shape[-2:]
    piece = jax.ShapeDtypeStruct((width // LANES, half // chips, LANES), jnp.bfloat16)
    shared = len(series) == 1
    return pl.pallas_call(
        functools.partial(apply_kernel, chips, shared, done),
        out_shape=jax.ShapeDtypeStruct((chips, *piece.shape), piece.dtype) if shared else [piece] * chips,
        compiler_params=pltpu.CompilerParams(vmem_limit_bytes=16 * MIB),
        name="apply_filter",
    )(high, low, *series, *begun)


def anomaly_kernel(chunks, chips, masked_ref, *refs):
    pieces, whole_ref, (out_ref, table, held, made, sems) = refs[:chips], refs[chips], refs[chips + 1 :]
    bands, lines, cols = made.shape
    dates = table.shape[1]
    height = lines // dates
    blocks = cols // LANES
    chip = lax.axis_index(DATE) // 2
    def fetch(step):
        here = pl.ds(step * SUB * height, SUB * height)
        return pltpu.make_async_copy(masked_ref.at[0:bands, here], held.at[:, here], sems.at[step, bands])

    for step in range(dates // SUB):
        fetch(step).start()
    turn = back_matrix(chunks[0] + chunks[1], height)
    order, start = [], 0
    for c, rows in enumerate(chunks):
        units = whole_ref.shape[1] if c > 0 else pieces[0].shape[0]
        for m in range(chips):
            if c > 0:
                table[pl.ds(start + m * units, units)] = whole_ref[m]
            else:
                table[pl.ds(start + partner(m, chips) * units, units)] = pieces[m][...]
        order += [(start + i * bands, len(rows) * bands) for i in range(len(rows))]
        start += units * chips

    def store(step, b):
        here = pl.ds(step * SUB * height, SUB * height)
        return pltpu.make_async_copy(made.at[b, here], out_ref.at[b, here], sems.at[step, b])

    for step in range(dates // SUB):
        at = pl.ds(step * SUB, SUB)
        here = pl.ds(step * SUB * height, SUB * height)
        fetch(step).wait()
        for b in range(bands):
            seasonal = jnp.concatenate(
                [
                    jnp.concatenate([table[first + k * step_k + b, at, :] for k in range(blocks)], axis=1)
                    for first, step_k in order
                ],
                axis=0,
            )
            clear = held[b, here, :].astype(jnp.float32)
            made[b, here, :] = jnp.where(clear < CLOUD / 2, clear - product(turn, seasonal), 0.0)
            store(step, b).start()
    for step in range(dates // SUB):
        for b in range(bands):
            store(step, b).wait()


def anomaly(masked, height, chunks, pieces, chips):
    bands, cols = masked.shape[0] - 1, masked.shape[2]
    dates = pieces[0].shape[1]
    lines = dates * height
    return pl.pallas_call(
        functools.partial(anomaly_kernel, chunks, chips),
        in_specs=[pl.BlockSpec(memory_space=pltpu.HBM)] + [pl.BlockSpec(memory_space=pltpu.VMEM)] * len(pieces),
        out_specs=pl.BlockSpec(memory_space=pl.ANY),
        out_shape=jax.ShapeDtypeStruct((bands, lines, cols), jnp.float32),
        scratch_shapes=[
            pltpu.VMEM((bands * cols // LANES * height, dates, LANES), jnp.bfloat16),
            pltpu.VMEM((bands, lines, cols), jnp.bfloat16),
            pltpu.VMEM((bands, lines, cols), jnp.float32),
            pltpu.SemaphoreType.DMA((dates // SUB, bands + 1)),
        ],
        compiler_params=pltpu.CompilerParams(vmem_limit_bytes=20 * MIB),
        name="anomaly",
    )(pltpu.with_memory_space_constraint(masked, pltpu.HBM), *pieces)


def exchange(pieces, peers):
    out = list(pieces)
    for m in range(len(pieces) - 1, 0, -1):
        to = [(i, i ^ (2 * apart(m, len(pieces), i % 2))) for i in range(peers)]
        out[m] = lax.ppermute(pieces[m], DATE, to)
    return out


def on_device(reflectance, clear_sky, harmonics):
    bands, dates, height, cols = reflectance.shape
    peers, tiles = lax.axis_size(DATE), lax.axis_size(TILE)
    chips = peers // 2
    clear = jnp.transpose(clear_sky, (1, 2, 0))
    chunks = (tuple(range(1, height - 1)), (height - 1, 0))
    refl = reflectance.reshape(bands, dates * height, cols)
    out = smooth_first(refl, clear, chunks, chips)
    masked, first, last = out[chips:]
    inner = exchange(out[:chips], peers)
    first, last = hand_on(first, last)
    up = [(i, i + 1) for i in range(tiles - 1)]
    before = lax.ppermute(last, TILE, up)
    after = lax.ppermute(first, TILE, [(j, i) for i, j in up])
    edges = smooth_rest(masked, height, (before, after), chunks[1], chips)
    outer = exchange(edges, peers)
    high, low = filter_matrix(harmonics, dates, peers)
    begun = begin(high, low, inner[:2])
    own = pack(inner, (begun, edges[0]), 1)
    other = lax.ppermute(own, DATE, [(i, i ^ 1) for i in range(peers)])
    made = apply_filter(high, low, (own, other), chips, (begun,), 2)
    results = exchange(made, peers)
    own = pack(outer, (made[0],), 2)
    both = lax.all_to_all(own, DATE, 0, 0, axis_index_groups=[[i, i + 1] for i in range(0, peers, 2)])
    made = apply_filter(high, low, (both,), chips)
    cores = [list(range(core, peers, 2)) for core in range(2)]
    results.append(lax.all_to_all(made, DATE, 0, 0, axis_index_groups=cores))
    return anomaly(masked, height, chunks, results, chips).reshape(reflectance.shape)


def solution(mesh):
    return jax.shard_map(
        on_device,
        mesh=mesh,
        in_specs=(P(None, DATE, TILE, None), P(DATE, TILE, None), P()),
        out_specs=P(None, DATE, TILE, None),
        check_vma=False,
    )
```

```python
import functools
import math

import jax
import jax.numpy as jnp
from jax import lax
from jax.experimental import pallas as pl
from jax.experimental.pallas import tpu as pltpu
from jax.sharding import PartitionSpec as P

LANES = 128
SUB = 32
MIB = 2**20
CLOUD = 1e30
DATE, TILE = ("date", "tile")


def apart(m, chips, core):
    bits = (chips - m) % chips
    width = chips.bit_length() - 1
    return sum((bits >> k & 1) << (width - 1 - k) for k in range(width)) if core else bits


def partner(m, chips, side=0):
    me = lax.axis_index(DATE)
    return (me // 2) ^ jnp.where(me % 2 == side, apart(m, chips, 0), apart(m, chips, 1))


def padded(size):
    return -(-size // LANES) * LANES


def turn_flags(clear_ref, flags_in, flags):
    height, blocks, dates = clear_ref.shape
    flags_in[...] = jnp.zeros_like(flags_in)
    for q in range(height):
        flags_in[q * blocks : (q + 1) * blocks, 0:dates] = clear_ref[q].astype(jnp.float32)
    flags[...] = flags_in[...].T.astype(jnp.bfloat16)


def grid_of(shape):
    return lax.broadcasted_iota(jnp.int32, shape, 0), lax.broadcasted_iota(jnp.int32, shape, 1)


def table_of(index, values):
    out = jnp.zeros_like(index)
    for i, value in enumerate(values):
        out = jnp.where(index == i, value, out)
    return out


def as_matrix(choice):
    return jnp.where(choice, 1.0, 0.0).astype(jnp.bfloat16)


def product(left, right):
    return jnp.dot(left, right, preferred_element_type=jnp.float32)


def add_row(lines, place, extra):
    parts = [lines[i : i + SUB] for i in range(0, lines.shape[0], SUB)]
    parts[place] = parts[place] + extra
    return jnp.concatenate(parts, axis=0)


def cover_matrices(height, blocks, width):
    line, date = grid_of((SUB * height, SUB))
    repeat = as_matrix(lax.div(line, height) == date)
    line, lane = grid_of((SUB * height, width))
    own = lax.rem(line, height) == lax.div(lane, blocks)
    lane, column = grid_of((width, blocks * LANES))
    columns = as_matrix(lax.rem(lane, blocks) == lax.div(column, LANES))
    return repeat, own, columns


def box_columns(blocks, width):
    lane, column = grid_of((width, blocks * LANES))
    total = jnp.zeros(lane.shape, jnp.float32)
    for shift in (-1, 0, 1):
        at = column + shift
        there = jnp.where(at < 0, -1, lax.div(at, LANES))
        total = total + jnp.where(there == lax.rem(lane, blocks), 1.0, 0.0)
    return total.astype(jnp.bfloat16)


def flag_lines(clear, repeat, own):
    return jnp.where(own, product(repeat, clear), 0.0).astype(jnp.bfloat16)


def turn_matrix(rows, height):
    line, source = grid_of((len(rows) * SUB, SUB * height))
    apart = jnp.abs(table_of(lax.div(line, SUB), rows) - lax.rem(source, height))
    return as_matrix((lax.rem(line, SUB) == lax.div(source, height)) & (apart <= 1))


def back_matrix(rows, height):
    line, source = grid_of((SUB * height, len(rows) * SUB))
    row = table_of(lax.div(source, SUB), rows)
    return as_matrix((lax.div(line, height) == lax.rem(source, SUB)) & (lax.rem(line, height) == row))


class Shelf:
    def __init__(self, rows, height, blocks, dates):
        width = padded(height * blocks)
        lines = len(rows) * SUB
        start = dates * height
        self.box = (pl.ds(start, width), pl.ds(0, blocks * LANES))
        start += width
        self.near = [(pl.ds(start + step * lines, lines), pl.ds(0, width)) for step in range(dates // SUB)]
        self.turn = (pl.ds(start, lines), pl.ds(width, SUB * height))
        self.size = start + dates // SUB * lines


def smooth_lines(down, scale, lane):
    cols = down.shape[1]
    west, east = pltpu.roll(down, 1, 1), pltpu.roll(down, cols - 1, 1)
    lane = lane[:, :LANES]
    west = jnp.concatenate([jnp.where(lane == 0, 0.0, west[:, :LANES]), west[:, LANES:]], axis=1)
    east = jnp.concatenate([east[:, :-LANES], jnp.where(lane == LANES - 1, 0.0, east[:, -LANES:])], axis=1)
    return ((down + west + east) * scale).astype(jnp.bfloat16)


def file_lines(table, at, smoothed, rows, b, bands):
    blocks = smoothed.shape[1] // LANES
    for k in range(blocks):
        for i in range(len(rows)):
            part = smoothed[i * SUB : (i + 1) * SUB, k * LANES : (k + 1) * LANES]
            table[(k * len(rows) + i) * bands + b, at, :] = part


def give_pieces(table, pieces):
    units = table.shape[0] // len(pieces)
    for m, piece in enumerate(pieces):
        piece[...] = table[pl.ds(partner(m, len(pieces)) * units, units)]


def first_kernel(chunks, chips, refl_ref, clear_ref, *refs):
    pieces, refs = refs[:chips], refs[chips:]
    masked_ref, first_ref, last_ref = refs[:3]
    table, held_ref, clear_held, flags_in, flags, sems = refs[3:]
    rows, rest = chunks
    bands, lines_all, cols = refl_ref.shape
    dates = pieces[0].shape[1]
    height = lines_all // dates
    shelf_ref = masked_ref.at[bands]
    blocks = cols // LANES
    flat = bands * blocks
    width = flags.shape[1]
    shelf = Shelf(rest, height, blocks, dates)

    def fetch(step):
        at = pl.ds(step * SUB * height, SUB * height)
        return pltpu.make_async_copy(refl_ref.at[:, at], held_ref.at[:, at], sems.at[step])

    fetch_clear = pltpu.make_async_copy(clear_ref, clear_held, sems.at[dates // SUB])
    fetch_clear.start()
    for step in range(dates // SUB):
        fetch(step).start()
    line, source = grid_of((2 * SUB, SUB * height))
    edge = jnp.where(line < SUB, 0, height - 1)
    edges = as_matrix((lax.rem(line, SUB) == lax.div(source, height)) & (edge == lax.rem(source, height)))
    flag_lane = lax.broadcasted_iota(jnp.int32, (SUB, width), 1)
    repeat, own, columns = cover_matrices(height, blocks, width)
    box = box_columns(blocks, width)
    turn = turn_matrix(rows, height)
    turn_rest = turn_matrix(rest, height)
    shelf_ref[shelf.box] = box
    shelf_ref[shelf.turn] = turn_rest
    lane = lax.broadcasted_iota(jnp.int32, (len(rows) * SUB, cols), 1)
    fetch_clear.wait()
    turn_flags(clear_held, flags_in, flags)

    for step in range(dates // SUB):
        at = pl.ds(step * SUB, SUB)
        here = pl.ds(step * SUB * height, SUB * height)
        clear = flags[at, :]
        lines = flag_lines(clear, repeat, own)
        cover = product(lines, columns).astype(jnp.bfloat16)
        shelf_ref[here, :] = cover
        for q, ref in ((0, first_ref), (height - 1, last_ref)):
            kept = jnp.where(lax.div(flag_lane, blocks) == q, clear.astype(jnp.float32), 0.0)
            ref[flat, at, :] = kept.astype(jnp.bfloat16)
        shelf_ref[shelf.near[step]] = product(turn_rest, lines).astype(jnp.bfloat16)
        count = product(product(turn, lines).astype(jnp.bfloat16), box)
        scale = 1.0 / jnp.maximum(count, 1.0)
        cloud = CLOUD - CLOUD * cover
        fetch(step).wait()
        for b in range(bands):
            masked = held_ref[b, here, :] * cover
            masked_ref[b, here, :] = masked + cloud
            ends = product(edges, masked).astype(jnp.bfloat16)
            for i, ref in enumerate((first_ref, last_ref)):
                for k in range(blocks):
                    ref[b * blocks + k, at, :] = ends[i * SUB : (i + 1) * SUB, k * LANES : (k + 1) * LANES]
            file_lines(table, at, smooth_lines(product(turn, masked), scale, lane), rows, b, bands)
    give_pieces(table, pieces)


def smooth_first(refl, clear, chunks, chips):
    bands, lines, cols = refl.shape
    height, blocks, dates = clear.shape
    number = bands * blocks * len(chunks[0])
    width = padded(height * blocks)
    pieces = [jax.ShapeDtypeStruct((number // chips, dates, LANES), jnp.bfloat16)] * chips
    size = Shelf(chunks[1], height, blocks, dates).size
    held = [pltpu.VMEM((bands + 1, size, cols), jnp.bfloat16)]
    edges = [jax.ShapeDtypeStruct((bands * blocks + 1, dates, width), jnp.bfloat16)] * 2
    return pl.pallas_call(
        functools.partial(first_kernel, chunks, chips),
        in_specs=[pl.BlockSpec(memory_space=pltpu.HBM)] * 2,
        out_specs=[pl.BlockSpec(memory_space=pltpu.VMEM)] * (chips + 3),
        out_shape=pieces + held + edges,
        scratch_shapes=[
            pltpu.VMEM((number, dates, LANES), jnp.bfloat16),
            pltpu.VMEM(refl.shape, refl.dtype),
            pltpu.VMEM(clear.shape, clear.dtype),
            pltpu.VMEM((width, padded(dates)), jnp.float32),
            pltpu.VMEM((padded(dates), width), jnp.bfloat16),
            pltpu.SemaphoreType.DMA((dates // SUB + 1,)),
        ],
        compiler_params=pltpu.CompilerParams(vmem_limit_bytes=14 * MIB),
        name="smooth_first",
    )(pltpu.with_memory_space_constraint(refl, pltpu.HBM), pltpu.with_memory_space_constraint(clear, pltpu.HBM))


def rest_kernel(rows, chips, height, masked_ref, before_ref, after_ref, *refs):
    pieces, table = refs[:chips], refs[chips]
    bands, cols = masked_ref.shape[0] - 1, masked_ref.shape[2]
    dates = pieces[0].shape[1]
    blocks = cols // LANES
    flat = bands * blocks
    shelf_ref = masked_ref.at[bands]
    shelf = Shelf(rows, height, blocks, dates)
    halo = tuple((rows.index(q), ref) for q, ref in ((0, before_ref), (height - 1, after_ref)))
    box, turn = shelf_ref[shelf.box], shelf_ref[shelf.turn]
    lane = lax.broadcasted_iota(jnp.int32, (len(rows) * SUB, cols), 1)
    for step in range(dates // SUB):
        at = pl.ds(step * SUB, SUB)
        here = pl.ds(step * SUB * height, SUB * height)
        count = product(shelf_ref[shelf.near[step]], box)
        for place, ref in halo:
            count = add_row(count, place, product(ref[flat, at, :], box))
        scale = 1.0 / jnp.maximum(count, 1.0)
        for b in range(bands):
            down = product(turn, masked_ref[b, here, :] * shelf_ref[here, :])
            for place, ref in halo:
                extra = jnp.concatenate([ref[b * blocks + k, at, :] for k in range(blocks)], axis=1)
                down = add_row(down, place, extra.astype(jnp.float32))
            file_lines(table, at, smooth_lines(down, scale, lane), rows, b, bands)
    give_pieces(table, pieces)


def hand_on_kernel(first_in, last_in, first_out, last_out):
    first_out[...] = first_in[...]
    last_out[...] = last_in[...]


def hand_on(first, last):
    return pl.pallas_call(
        hand_on_kernel,
        out_shape=[jax.ShapeDtypeStruct(x.shape, x.dtype) for x in (first, last)],
        compiler_params=pltpu.CompilerParams(vmem_limit_bytes=8 * MIB),
        name="hand_on",
    )(first, last)


def smooth_rest(masked, height, halo, rows, chips):
    bands, cols = masked.shape[0] - 1, masked.shape[2]
    dates = halo[0].shape[1]
    number = bands * (cols // LANES) * len(rows)
    return pl.pallas_call(
        functools.partial(rest_kernel, rows, chips, height),
        in_specs=[pl.BlockSpec(memory_space=pltpu.VMEM)] * 3,
        out_shape=[jax.ShapeDtypeStruct((number // chips, dates, LANES), jnp.bfloat16)] * chips,
        scratch_shapes=[pltpu.VMEM((number, dates, LANES), jnp.bfloat16)],
        compiler_params=pltpu.CompilerParams(vmem_limit_bytes=12 * MIB),
        name="smooth_rest",
    )(masked, *halo)


def filter_kernel(dates, wave_ref, high_ref, low_ref, turned):
    total = high_ref.shape[1]
    chips = total // dates // 2
    core = lax.axis_index(DATE) % 2
    wave = jnp.concatenate(
        [jnp.broadcast_to(wave_ref[a : a + 1, :], (dates, LANES)) for a in range(total // LANES)], axis=1
    )
    same = pltpu.roll(wave, 0, 1, stride=1, stride_axis=0)
    other = jnp.where(core == 0, pltpu.roll(same, total - dates, 1), pltpu.roll(same, dates, 1))
    for side, base in enumerate((same, other)):
        high = base.astype(jnp.bfloat16)
        low = (base - high.astype(jnp.float32)).astype(jnp.bfloat16)
        for n, (ref, part) in enumerate(((high_ref, high), (low_ref, low))):
            turned[2 * side + n] = part
            for m in range(chips):
                for q in range(chips):
                    step = lax.rem(partner(m, chips, side) + chips - q, chips)
                    at = pl.multiple_of(step * 2 * dates, LANES)
                    left = (side * chips + m) * dates
                    ref[q * dates : (q + 1) * dates, left : left + dates] = turned[2 * side + n, :, pl.ds(at, dates)]


def filter_matrix(harmonics, dates, peers):
    total = dates * peers
    fine = jnp.arange(LANES, dtype=jnp.int32)
    coarse = jnp.arange(0, total, LANES, dtype=jnp.int32)

    def turned(steps):
        angle = (harmonics[:, None] * steps[None, :] % total).astype(jnp.float32) * (2.0 * math.pi / total)
        return jnp.cos(angle), jnp.sin(angle)

    (cos_a, sin_a), (cos_b, sin_b) = turned(coarse), turned(fine)
    wave = jnp.einsum(
        "fa,fb->ab",
        jnp.concatenate([cos_a, sin_a], axis=0),
        jnp.concatenate([cos_b, -sin_b], axis=0),
        precision=lax.Precision.HIGHEST,
    )
    wave = wave * (2.0 / total)
    return pl.pallas_call(
        functools.partial(filter_kernel, dates),
        out_shape=[jax.ShapeDtypeStruct((total // 2, total), jnp.bfloat16)] * 2,
        scratch_shapes=[pltpu.VMEM((4, dates, total), jnp.bfloat16)],
        compiler_params=pltpu.CompilerParams(vmem_limit_bytes=10 * MIB),
        name="filter_matrix",
    )(wave)


def pack_kernel(chips, *refs):
    pieces, out_ref = refs[:chips], refs[-1]
    units, dates, lanes = pieces[0].shape
    for m in range(chips):
        at = m * dates
        for i in range(units):
            part = (pl.ds(at, dates), pl.ds(i * lanes, lanes))
            for side in ((0,), (1,)) if len(out_ref.shape) == 3 else ((),):
                out_ref[side + part] = pieces[m][i]


def pack(pieces, after, copies):
    units, dates, lanes = pieces[0].shape
    shape = (len(pieces) * dates, units * lanes)
    return pl.pallas_call(
        functools.partial(pack_kernel, len(pieces)),
        in_specs=[pl.BlockSpec(memory_space=pltpu.VMEM)] * len(pieces)
        + [pl.BlockSpec(memory_space=pl.ANY)] * len(after),
        out_shape=jax.ShapeDtypeStruct((copies, *shape) if copies > 1 else shape, jnp.bfloat16),
        compiler_params=pltpu.CompilerParams(vmem_limit_bytes=8 * MIB),
        name="pack",
    )(*pieces, *after)


def begin_kernel(high_ref, low_ref, *refs):
    pieces, (result, series) = refs[:-2], refs[-2:]
    units, dates, lanes = pieces[0].shape
    for m, piece in enumerate(pieces):
        for i in range(units):
            series[m * dates : (m + 1) * dates, i * lanes : (i + 1) * lanes] = piece[i]
    depth, tile = series.shape[0], dates
    for at in range(0, result.shape[0], tile):
        lines = pl.ds(at, tile)
        result[lines, :] = product(high_ref[lines, :depth], series[...]) + product(low_ref[lines, :depth], series[...])


def begin(high, low, pieces):
    units, dates, lanes = pieces[0].shape
    return pl.pallas_call(
        begin_kernel,
        out_shape=jax.ShapeDtypeStruct((high.shape[0], units * lanes), jnp.float32),
        scratch_shapes=[pltpu.VMEM((len(pieces) * dates, units * lanes), jnp.bfloat16)],
        compiler_params=pltpu.CompilerParams(vmem_limit_bytes=12 * MIB),
        name="begin",
    )(high, low, *pieces)


def apply_kernel(chips, shared, done, high_ref, low_ref, *refs):
    outs = refs[-1] if shared else refs[-chips:]
    units, dates, lanes = outs.shape[1:] if shared else outs[0].shape
    half = high_ref.shape[0]
    core = lax.axis_index(DATE) % 2
    own_ref, other_ref = (refs[0].at[core], refs[0].at[1 - core]) if shared else refs[:2]
    begun = done * dates
    for m in range(chips):
        at = pl.ds(m * dates if shared else pl.multiple_of(partner(m, chips) * dates, dates), dates)
        out = outs.at[m] if shared else outs[m]
        total = refs[2][at, :] if done > 0 else None
        for ref in (high_ref, low_ref):
            for series, first, left in ((own_ref, begun, 0), (other_ref, 0, half)):
                part = product(ref[at, left + first : left + half], series[first:half, :])
                total = part if total is None else total + part
        for i in range(units):
            out[i] = total[:, i * lanes : (i + 1) * lanes].astype(jnp.bfloat16)


def apply_filter(high, low, series, chips, begun=(), done=0):
    half, width = series[0].shape[-2:]
    piece = jax.ShapeDtypeStruct((width // LANES, half // chips, LANES), jnp.bfloat16)
    shared = len(series) == 1
    return pl.pallas_call(
        functools.partial(apply_kernel, chips, shared, done),
        out_shape=jax.ShapeDtypeStruct((chips, *piece.shape), piece.dtype) if shared else [piece] * chips,
        compiler_params=pltpu.CompilerParams(vmem_limit_bytes=16 * MIB),
        name="apply_filter",
    )(high, low, *series, *begun)


def anomaly_kernel(chunks, chips, masked_ref, *refs):
    pieces, whole_ref, (out_ref, table, held, made, sems) = refs[:chips], refs[chips], refs[chips + 1 :]
    bands, lines, cols = made.shape
    dates = table.shape[1]
    height = lines // dates
    blocks = cols // LANES
    chip = lax.axis_index(DATE) // 2
    def fetch(step):
        here = pl.ds(step * SUB * height, SUB * height)
        return pltpu.make_async_copy(masked_ref.at[0:bands, here], held.at[:, here], sems.at[step, bands])

    for step in range(dates // SUB):
        fetch(step).start()
    turn = back_matrix(chunks[0] + chunks[1], height)
    order, start = [], 0
    for c, rows in enumerate(chunks):
        units = whole_ref.shape[1] if c > 0 else pieces[0].shape[0]
        for m in range(chips):
            if c > 0:
                table[pl.ds(start + m * units, units)] = whole_ref[m]
            else:
                table[pl.ds(start + partner(m, chips) * units, units)] = pieces[m][...]
        order += [(start + i * bands, len(rows) * bands) for i in range(len(rows))]
        start += units * chips

    def store(step, b):
        here = pl.ds(step * SUB * height, SUB * height)
        return pltpu.make_async_copy(made.at[b, here], out_ref.at[b, here], sems.at[step, b])

    for step in range(dates // SUB):
        at = pl.ds(step * SUB, SUB)
        here = pl.ds(step * SUB * height, SUB * height)
        fetch(step).wait()
        for b in range(bands):
            seasonal = jnp.concatenate(
                [
                    jnp.concatenate([table[first + k * step_k + b, at, :] for k in range(blocks)], axis=1)
                    for first, step_k in order
                ],
                axis=0,
            )
            clear = held[b, here, :].astype(jnp.float32)
            made[b, here, :] = jnp.where(clear < CLOUD / 2, clear - product(turn, seasonal), 0.0)
            store(step, b).start()
    for step in range(dates // SUB):
        for b in range(bands):
            store(step, b).wait()


def anomaly(masked, height, chunks, pieces, chips):
    bands, cols = masked.shape[0] - 1, masked.shape[2]
    dates = pieces[0].shape[1]
    lines = dates * height
    return pl.pallas_call(
        functools.partial(anomaly_kernel, chunks, chips),
        in_specs=[pl.BlockSpec(memory_space=pltpu.HBM)] + [pl.BlockSpec(memory_space=pltpu.VMEM)] * len(pieces),
        out_specs=pl.BlockSpec(memory_space=pl.ANY),
        out_shape=jax.ShapeDtypeStruct((bands, lines, cols), jnp.float32),
        scratch_shapes=[
            pltpu.VMEM((bands * cols // LANES * height, dates, LANES), jnp.bfloat16),
            pltpu.VMEM((bands, lines, cols), jnp.bfloat16),
            pltpu.VMEM((bands, lines, cols), jnp.float32),
            pltpu.SemaphoreType.DMA((dates // SUB, bands + 1)),
        ],
        compiler_params=pltpu.CompilerParams(vmem_limit_bytes=20 * MIB),
        name="anomaly",
    )(pltpu.with_memory_space_constraint(masked, pltpu.HBM), *pieces)


def exchange(pieces, peers):
    out = list(pieces)
    for m in range(len(pieces) - 1, 0, -1):
        to = [(i, i ^ (2 * apart(m, len(pieces), i % 2))) for i in range(peers)]
        out[m] = lax.ppermute(pieces[m], DATE, to)
    return out


def on_device(reflectance, clear_sky, harmonics):
    bands, dates, height, cols = reflectance.shape
    peers, tiles = lax.axis_size(DATE), lax.axis_size(TILE)
    chips = peers // 2
    clear = jnp.transpose(clear_sky, (1, 2, 0))
    chunks = (tuple(range(1, height - 1)), (height - 1, 0))
    refl = reflectance.reshape(bands, dates * height, cols)
    out = smooth_first(refl, clear, chunks, chips)
    masked, first, last = out[chips:]
    inner = exchange(out[:chips], peers)
    first, last = hand_on(first, last)
    up = [(i, i + 1) for i in range(tiles - 1)]
    before = lax.ppermute(last, TILE, up)
    after = lax.ppermute(first, TILE, [(j, i) for i, j in up])
    edges = smooth_rest(masked, height, (before, after), chunks[1], chips)
    outer = exchange(edges, peers)
    high, low = filter_matrix(harmonics, dates, peers)
    begun = begin(high, low, inner[:2])
    own = pack(inner, (begun, edges[0]), 1)
    other = lax.ppermute(own, DATE, [(i, i ^ 1) for i in range(peers)])
    made = apply_filter(high, low, (own, other), chips, (begun,), 2)
    results = exchange(made, peers)
    own = pack(outer, (made[0],), 2)
    both = lax.all_to_all(own, DATE, 0, 0, axis_index_groups=[[i, i + 1] for i in range(0, peers, 2)])
    made = apply_filter(high, low, (both,), chips)
    cores = [list(range(core, peers, 2)) for core in range(2)]
    results.append(lax.all_to_all(made, DATE, 0, 0, axis_index_groups=cores))
    return anomaly(masked, height, chunks, results, chips).reshape(reflectance.shape)


def solution(mesh):
    return jax.shard_map(
        on_device,
        mesh=mesh,
        in_specs=(P(None, DATE, TILE, None), P(DATE, TILE, None), P()),
        out_specs=P(None, DATE, TILE, None),
        check_vma=False,
    )
```
